32 devices in a mesh: gx: 16 (over z, y, x), gy: 2 (over core).
Axes of the slice: x: 2, y: 2, z: 4, core: 2. Of those that a mesh axis runs over, the one named last changes fastest.
Arguments:
- noisy: bfloat16 [2, 1024, 512], P(None, 'gx', 'gy'), may hold values from -6 to 6
- dilations: int32 [3], replicated, may hold values from 1 to 256, as said below
- conv_weights: float32 [3, 4, 27], replicated, may hold values from -0.625 to 0.625
- biases: float32 [3], replicated, may hold values from -3 to 3
- mix_weights: float32 [4], replicated, may hold values from -3 to 3
Outputs:
- denoised: bfloat16 [2, 1024, 512], P(None, 'gx', 'gy')
The draws below stay inside these ranges and needn't reach their ends.
Inputs may be any that keep to these rules, and one draw needn't show every extreme that they name: `dilations`: every layer's dilation lies in 1 .. 256; some layer has dilation 256.
All inputs are finite; a program needn't handle non-finite values.
Results may differ from the reference program's by a relative error of at most 0.0065.
Values sent between devices are 32-bit elements; how exact they have to be, the bound alone decides.
No kernel may reach another device: no remote copies, remote signals or barrier semaphores. Data moves between devices by JAX's collectives and lax.ppermute only.
A program may use at most 64 MiB of HBM per device.

```python
import jax
import jax.numpy as jnp
from jax import lax

Z = 2
LAYERS = 3
DMAX = 256
NX = 1024
NY = 512


def draw_dilations(key, part):
    first_key = jax.random.fold_in(key, 11)
    second_key = jax.random.fold_in(key, 23)
    values = jax.random.randint(first_key, (LAYERS,), 1, DMAX + 1)
    chosen = jax.random.randint(second_key, (), 0, LAYERS)
    return jnp.where(jnp.arange(LAYERS) == chosen, DMAX, values).astype(jnp.int32)


def level_of(stream_key, dims, pieces, smallest, high):
    def one(dim, parts):
        steps = jax.random.uniform(jax.random.fold_in(jax.random.fold_in(stream_key, 6), dim), (parts,), jnp.float32, smallest / len(pieces), high / len(pieces))
        return jnp.repeat(jnp.exp(steps), dims[dim] // parts).reshape((-1,) + (1,) * (len(dims) - dim - 1))

    factor_of = one(*pieces[0])
    for cut in pieces[1:]:
        factor_of = factor_of * one(*cut)
    return factor_of


def gaussian(own_key, dims, width, most, split=(), dtype=jnp.bfloat16):
    entries = jax.random.normal(own_key, dims, jnp.float32) * width
    if len(split) > 0:
        entries = level_of(own_key, dims, split, -0.22, 0.18) * entries
    return jnp.clip(entries, min=-most, max=most).astype(dtype)


def setup_inputs(seed: int = 0) -> dict:
    key_list = jax.random.split(jax.random.key(seed), 6)
    return {
        "noisy": gaussian(key_list[0], (Z, NX, NY), 1.0, 6.0, ((1, 16), (2, 2))),
        "dilations": draw_dilations(jax.random.fold_in(key_list[5], 71), 0),
        "conv_weights": gaussian(key_list[2], (LAYERS, LAYERS + 1, 27), (27 * LAYERS) ** -0.5, 0.625, (), jnp.float32),
        "biases": gaussian(key_list[3], (LAYERS,), 0.5, 3.0, (), jnp.float32),
        "mix_weights": gaussian(key_list[4], (LAYERS + 1,), (LAYERS + 1) ** -0.5, 3.0, (), jnp.float32),
    }


def shift_along(source_field, axis_index, offset):
    widths = [(0, 0)] * source_field.ndim
    widths[axis_index] = (DMAX, DMAX)
    padded = jnp.pad(source_field, widths)
    start_index = (offset + DMAX).astype(jnp.int32)
    return lax.dynamic_slice_in_dim(padded, start_index, source_field.shape[axis_index], axis_index)


def tap_sums(feature_maps, layer_weights):
    map_count = len(feature_maps)
    stacked = jnp.stack(feature_maps).astype(jnp.float32)
    padded = jnp.pad(stacked, ((0, 0), (1, 1), (0, 0), (0, 0)))
    depth = stacked.shape[1]
    zstack = jnp.stack([padded[:, shift_index:shift_index + depth] for shift_index in range(3)])
    kernel = layer_weights[:map_count].reshape(map_count, 3, 3, 3)
    return jnp.einsum("cjzxy,jcab->abzxy", zstack, kernel, precision=lax.Precision.HIGHEST,
                      preferred_element_type=jnp.float32)


def reference(noisy, dilations, conv_weights, biases, mix_weights):
    feature_maps = [noisy]
    for layer_index in range(LAYERS):
        reach = dilations[layer_index]
        partial_value = tap_sums(feature_maps, conv_weights[layer_index])
        summed = jnp.zeros(noisy.shape, jnp.float32)
        for row_tap in range(3):
            for col_tap in range(3):
                shifted = shift_along(partial_value[row_tap, col_tap], 1, (row_tap - 1) * reach)
                shifted = shift_along(shifted, 2, (col_tap - 1) * reach)
                summed = summed + shifted
        feature_maps.append(jax.nn.relu(summed + biases[layer_index]).astype(jnp.bfloat16))
    output = jnp.zeros(noisy.shape, jnp.float32)
    for map_index in range(LAYERS + 1):
        output = output + mix_weights[map_index] * feature_maps[map_index].astype(jnp.float32)
    return output.astype(jnp.bfloat16)
```

```python
import functools

import jax
import jax.numpy as jnp
from jax import lax
from jax.experimental import pallas as pl
from jax.experimental.pallas import tpu as pltpu
from jax.sharding import PartitionSpec as P

DMAX = 256
ROWS = 32
CHUNK = 16
SMEM = pl.BlockSpec(memory_space=pltpu.SMEM)
VMEM = pl.BlockSpec(memory_space=pltpu.VMEM)


def pair_gather(value):
    count = lax.axis_size("gy")
    groups = None if count == 2 else [[i, i + 1] for i in range(0, count, 2)]
    return lax.all_gather(value, "gy", axis=0, axis_index_groups=groups)


def widen(field):
    count = lax.axis_size("gy")
    if count == 2:
        return field
    height = field.shape[-1] // 2
    before = lax.ppermute(field[..., height:], "gy", [(i, i + 2) for i in range(count - 2)])
    after = lax.ppermute(field[..., :height], "gy", [(i + 2, i) for i in range(count - 2)])
    return jnp.concatenate([before, field, after], axis=-1)


def outward(value, steps):
    blocks, columns = lax.axis_size("gx"), lax.axis_size("gy")
    moves = []
    for k in range(blocks):
        for g in range(columns):
            target = k - steps if g % 2 == 0 else k + steps
            if 0 <= target < blocks:
                moves.append((k * columns + g, target * columns + g))
    return lax.ppermute(value, ("gx", "gy"), moves)


def branch_counts(width):
    most = -(-DMAX // width)
    parts = width // CHUNK
    return most, parts, most * parts + most


def routes(dilations, width):
    most, parts, total = branch_counts(width)
    bits = total.bit_length()
    route = jnp.where(
        lax.rem(dilations, width) == 0,
        most * parts - 1 + lax.div(dilations, width),
        lax.div(dilations - 1, CHUNK),
    )
    layers = dilations.shape[0]
    packed = jnp.sum(route << (bits * jnp.arange(layers, dtype=jnp.int32)), dtype=jnp.int32)
    return [(packed >> (bits * layer)) & ((1 << bits) - 1) for layer in range(layers)]


def exchange(sent, beside, route):
    width = sent.shape[1]
    most, parts, _ = branch_counts(width)

    def straddling(blocks, part, sent, others):
        near = sent[:, : width - part * CHUNK]
        if blocks > 0:
            near = outward(near, blocks)
        far = outward(sent[:, width - (part + 1) * CHUNK :], blocks + 1)
        made = beside[0](*others)
        return pair_gather(jnp.concatenate([near, far], axis=1)), made

    def exact(blocks, sent, others):
        near = outward(sent, blocks)
        made = beside[0](*others)
        return pair_gather(jnp.concatenate([near, jnp.zeros_like(near[:, :CHUNK])], axis=1)), made

    branches = [
        functools.partial(straddling, blocks, part) for blocks in range(most) for part in range(parts)
    ]
    branches += [functools.partial(exact, blocks) for blocks in range(1, most + 1)]
    return lax.switch(route, branches, sent, beside[1])


def tap_rows(layer, a, maps, weights, reach, rows, halo):
    depth, _, wide = maps[0].shape
    inner = wide - 2 * halo
    loaded = [[ref[z, rows, :].astype(jnp.float32) for z in range(depth)] for ref in maps]
    column = lax.broadcasted_iota(jnp.int32, (loaded[0][0].shape[0], inner), 1)
    sums = []
    for z in range(depth):
        total = None
        for b in (-1, 0, 1):
            part = None
            for j, planes in enumerate(loaded):
                for c in (-1, 0, 1):
                    if 0 <= z + c < depth:
                        weight = weights[layer, j, 9 * (c + 1) + 3 * (a + 1) + (b + 1)]
                        term = weight * planes[z + c]
                        part = term if part is None else part + term
            if b == 1:
                part = pltpu.roll(part, wide - reach, 1)
            elif b == -1:
                part = pltpu.roll(part, reach, 1)
            part = part[:, halo : halo + inner]
            if halo == 0 and b == 1:
                part = jnp.where(column < inner - reach, part, 0.0)
            elif halo == 0 and b == -1:
                part = jnp.where(column >= reach, part, 0.0)
            total = part if total is None else total + part
        sums.append(total)
    return sums


def sent_body(layer, maps, weights, dilations, sent, halo):
    depth, width, _ = sent.shape
    reach = dilations[layer]
    side = lax.rem(lax.axis_index("gy"), 2)

    @pl.loop(0, width, step=ROWS)
    def _(first):
        rows = pl.ds(pl.multiple_of(first, ROWS), ROWS)
        for z, plane in enumerate(tap_rows(layer, 1 - 2 * side, maps, weights, reach, rows, halo)):
            sent[z, rows, :] = plane

    @pl.when(side == 0)
    def _():
        turn = lax.rem(width - lax.rem(reach, width), width)
        for z in range(depth):
            sent[z] = pltpu.roll(sent[z], turn, 0)


def map_body(layer, came, centre, dilations, biases, made):
    depth, width, _ = centre.shape
    turn = lax.rem(dilations[layer], width)
    row = lax.broadcasted_iota(jnp.int32, centre.shape[1:], 0)
    for z in range(depth):
        upper, lower = (
            jnp.where(row < width - turn, came[side, z, :width], came[side, z, CHUNK:]) for side in (0, 1)
        )
        total = centre[z] + upper + pltpu.roll(lower, turn, 0) + biases[layer]
        made[z] = jnp.maximum(total, 0.0).astype(jnp.bfloat16).astype(jnp.float32)


def own_half(ref_shape, write):
    half = ref_shape[-1]
    side = lax.rem(lax.axis_index("gy"), 2)
    for member in (0, 1):
        pl.when(side == member)(functools.partial(write, slice(member * half, (member + 1) * half)))


def first_kernel(dilations, weights, came, made, sent):
    height = came.shape[-1]
    made[:, :, :height] = came[0]
    made[:, :, height:] = came[1]
    sent_body(0, [made], weights, dilations, sent, 0)


def sent_kernel(layer, halo, dilations, weights, *refs):
    sent_body(layer, refs[:-1], weights, dilations, refs[-1], halo)


def map_kernel(layer, dilations, biases, came, centre, made):
    map_body(layer, came, centre, dilations, biases, made)


def layer_kernel(layer, dilations, weights, biases, came, centre, *refs):
    maps, (made, sent) = refs[:layer], refs[layer:]
    map_body(layer - 1, came, centre, dilations, biases, made)
    sent_body(layer, [*maps, made], weights, dilations, sent, 0)


def last_kernel(layers, dilations, biases, mix, came, centre, mixed, out, made):
    map_body(layers - 1, came, centre, dilations, biases, made)

    def write(columns):
        out[...] = (mixed[...] + mix[layers] * made[:, :, columns]).astype(jnp.bfloat16)

    own_half(out.shape, write)


def beside_kernel(layer, last, halo, dilations, weights, mix, *refs):
    maps, (centre, kept) = refs[: layer + 1], refs[layer + 1 :]
    _, width, inner = centre.shape
    reach = dilations[layer]

    @pl.loop(0, width, step=ROWS)
    def _(first):
        rows = pl.ds(pl.multiple_of(first, ROWS), ROWS)
        for z, plane in enumerate(tap_rows(layer, 0, maps, weights, reach, rows, halo)):
            centre[z, rows, :] = plane

    if not last:
        kept[...] = maps[-1][...].astype(jnp.bfloat16)
        return

    def write(columns):
        columns = slice(columns.start + halo, columns.stop + halo)
        kept[...] = sum(mix[j] * ref[:, :, columns].astype(jnp.float32) for j, ref in enumerate(maps))

    own_half(kept.shape, write)


def call(kernel, out_shape, scalars, arrays, scratch=(), cost=None):
    return pl.pallas_call(
        kernel,
        out_shape=out_shape,
        in_specs=[SMEM] * len(scalars) + [VMEM] * len(arrays),
        out_specs=jax.tree.map(lambda _: VMEM, out_shape),
        scratch_shapes=list(scratch),
        cost_estimate=cost,
    )(*scalars, *arrays)


def body(noisy, dilations, conv_weights, biases, mix_weights):
    layers = conv_weights.shape[0]
    depth, width, height = noisy.shape
    paired = lax.axis_size("gy") == 2
    halo = 0 if paired else height
    assert height >= DMAX and lax.axis_size("gy") % 2 == 0 and width % ROWS == 0
    field = jax.ShapeDtypeStruct((depth, width, 2 * height), jnp.float32)
    wide = (depth, width, 2 * (height + halo))
    own = jax.ShapeDtypeStruct(noisy.shape, jnp.float32)
    route = routes(dilations, width)
    cost = pl.CostEstimate(flops=72 * depth * width * 2 * height, bytes_accessed=1 << 20, transcendentals=0)

    def beside(layer, newest, older):
        last = layer == layers - 1
        shapes = (field, own if last else jax.ShapeDtypeStruct(wide, jnp.bfloat16))

        def run(dilations, weights, mix, *maps):
            return call(
                functools.partial(beside_kernel, layer, last, halo),
                shapes,
                (dilations, weights, mix),
                maps,
                cost=cost,
            )

        return run, (dilations, conv_weights, mix_weights, *older, newest)

    def send(layer, newest, older):
        return call(
            functools.partial(sent_kernel, layer, halo), field, (dilations, conv_weights), (*older, newest)
        )

    came = pair_gather(noisy.astype(jnp.float32))
    older = []
    if paired:
        newest, sent = call(first_kernel, (field, field), (dilations, conv_weights), (came,))
    else:
        newest = widen(jnp.concatenate([came[0], came[1]], axis=-1))
        sent = send(0, newest, older)
    for layer in range(1, layers):
        came, (centre, kept) = exchange(sent, beside(layer - 1, newest, older), route[layer - 1])
        older.append(kept)
        if paired:
            newest, sent = call(
                functools.partial(layer_kernel, layer),
                (field, field),
                (dilations, conv_weights, biases),
                (came, centre, *older),
            )
        else:
            newest = call(
                functools.partial(map_kernel, layer - 1), field, (dilations, biases), (came, centre)
            )
            newest = widen(newest)
            sent = send(layer, newest, older)
    came, (centre, mixed) = exchange(sent, beside(layers - 1, newest, older), route[layers - 1])
    return call(
        functools.partial(last_kernel, layers),
        jax.ShapeDtypeStruct(noisy.shape, jnp.bfloat16),
        (dilations, biases, mix_weights),
        (came, centre, mixed),
        scratch=[pltpu.VMEM(field.shape, jnp.float32)],
    )


def solution(mesh):
    return jax.shard_map(
        body,
        mesh=mesh,
        in_specs=(P(None, "gx", "gy"), P(), P(), P(), P()),
        out_specs=P(None, "gx", "gy"),
        check_vma=False,
    )
```

```python
import functools

import jax
import jax.numpy as jnp
from jax import lax
from jax.experimental import pallas as pl
from jax.experimental.pallas import tpu as pltpu
from jax.sharding import PartitionSpec as P

DMAX = 256
ROWS = 32
CHUNK = 16
SMEM = pl.BlockSpec(memory_space=pltpu.SMEM)
VMEM = pl.BlockSpec(memory_space=pltpu.VMEM)


def pair_gather(value):
    count = lax.axis_size("gy")
    groups = None if count == 2 else [[i, i + 1] for i in range(0, count, 2)]
    return lax.all_gather(value, "gy", axis=0, axis_index_groups=groups)


def widen(field):
    count = lax.axis_size("gy")
    if count == 2:
        return field
    height = field.shape[-1] // 2
    before = lax.ppermute(field[..., height:], "gy", [(i, i + 2) for i in range(count - 2)])
    after = lax.ppermute(field[..., :height], "gy", [(i + 2, i) for i in range(count - 2)])
    return jnp.concatenate([before, field, after], axis=-1)


def outward(value, steps):
    blocks, columns = lax.axis_size("gx"), lax.axis_size("gy")
    moves = []
    for k in range(blocks):
        for g in range(columns):
            target = k - steps if g % 2 == 0 else k + steps
            inside = 0 <= target < blocks
            moves.append((k * columns + g, target * columns + g if inside else k * columns + (g ^ 1)))
    return lax.ppermute(value, ("gx", "gy"), moves)


def branch_counts(width):
    most = -(-DMAX // width)
    parts = width // CHUNK
    return most, parts, most * parts + most


def routes(dilations, width):
    most, parts, total = branch_counts(width)
    bits = total.bit_length()
    route = jnp.where(
        lax.rem(dilations, width) == 0,
        most * parts - 1 + lax.div(dilations, width),
        lax.div(dilations - 1, CHUNK),
    )
    layers = dilations.shape[0]
    packed = jnp.sum(route << (bits * jnp.arange(layers, dtype=jnp.int32)), dtype=jnp.int32)
    packed = lax.optimization_barrier(packed - 1) + 1
    return [(packed >> (bits * layer)) & ((1 << bits) - 1) for layer in range(layers)]


def exchange(sent, beside, route):
    width = sent.shape[1]
    most, parts, _ = branch_counts(width)

    def straddling(blocks, part, sent, others):
        near = sent[:, : width - part * CHUNK]
        if blocks > 0:
            near = outward(near, blocks)
        far = outward(sent[:, width - (part + 1) * CHUNK :], blocks + 1)
        made = beside[0](*others)
        return pair_gather(jnp.concatenate([near, far], axis=1)), made

    def exact(blocks, sent, others):
        near = outward(sent, blocks)
        made = beside[0](*others)
        return pair_gather(jnp.concatenate([near, jnp.zeros_like(near[:, :CHUNK])], axis=1)), made

    branches = [
        functools.partial(straddling, blocks, part) for blocks in range(most) for part in range(parts)
    ]
    branches += [functools.partial(exact, blocks) for blocks in range(1, most + 1)]
    return lax.switch(route, branches, sent, beside[1])


def tap_rows(layer, a, maps, weights, reach, rows, halo):
    depth, _, wide = maps[0].shape
    inner = wide - 2 * halo
    loaded = [[ref[z, rows, :].astype(jnp.float32) for z in range(depth)] for ref in maps]
    column = lax.broadcasted_iota(jnp.int32, (loaded[0][0].shape[0], inner), 1)
    sums = []
    for z in range(depth):
        total = None
        for b in (-1, 0, 1):
            part = None
            for j, planes in enumerate(loaded):
                for c in (-1, 0, 1):
                    if 0 <= z + c < depth:
                        weight = weights[layer, j, 9 * (c + 1) + 3 * (a + 1) + (b + 1)]
                        term = weight * planes[z + c]
                        part = term if part is None else part + term
            if b == 1:
                part = pltpu.roll(part, wide - reach, 1)
            elif b == -1:
                part = pltpu.roll(part, reach, 1)
            part = part[:, halo : halo + inner]
            if halo == 0 and b == 1:
                part = jnp.where(column < inner - reach, part, 0.0)
            elif halo == 0 and b == -1:
                part = jnp.where(column >= reach, part, 0.0)
            total = part if total is None else total + part
        sums.append(total)
    return sums


def sent_body(layer, maps, weights, dilations, sent, halo):
    depth, width, _ = sent.shape
    reach = dilations[layer]
    side = lax.rem(lax.axis_index("gy"), 2)

    @pl.loop(0, width, step=ROWS)
    def _(first):
        rows = pl.ds(pl.multiple_of(first, ROWS), ROWS)
        for z, plane in enumerate(tap_rows(layer, 1 - 2 * side, maps, weights, reach, rows, halo)):
            sent[z, rows, :] = plane

    @pl.when(side == 0)
    def _():
        turn = lax.rem(width - lax.rem(reach, width), width)
        for z in range(depth):
            sent[z] = pltpu.roll(sent[z], turn, 0)


def map_body(layer, blocks, came, centre, dilations, biases, made):
    depth, width, _ = centre.shape
    reach = dilations[layer]
    turn = lax.rem(reach, width)
    block = lax.axis_index("gx")
    row = lax.broadcasted_iota(jnp.int32, centre.shape[1:], 0)
    for z in range(depth):
        upper, lower = (
            jnp.where(row < width - turn, came[side, z, :width], came[side, z, CHUNK:]) for side in (0, 1)
        )
        upper = jnp.where(row < (blocks - block) * width - reach, upper, 0.0)
        lower = jnp.where(row >= reach - block * width, pltpu.roll(lower, turn, 0), 0.0)
        total = centre[z] + upper + lower + biases[layer]
        made[z] = jnp.maximum(total, 0.0).astype(jnp.bfloat16).astype(jnp.float32)


def own_half(ref_shape, write):
    half = ref_shape[-1]
    side = lax.rem(lax.axis_index("gy"), 2)
    for member in (0, 1):
        pl.when(side == member)(functools.partial(write, slice(member * half, (member + 1) * half)))


def first_kernel(dilations, weights, came, made, sent):
    height = came.shape[-1]
    made[:, :, :height] = came[0]
    made[:, :, height:] = came[1]
    sent_body(0, [made], weights, dilations, sent, 0)


def sent_kernel(layer, halo, dilations, weights, *refs):
    sent_body(layer, refs[:-1], weights, dilations, refs[-1], halo)


def map_kernel(layer, blocks, dilations, biases, came, centre, made):
    map_body(layer, blocks, came, centre, dilations, biases, made)


def layer_kernel(layer, blocks, dilations, weights, biases, came, centre, *refs):
    maps, (made, sent) = refs[:layer], refs[layer:]
    map_body(layer - 1, blocks, came, centre, dilations, biases, made)
    sent_body(layer, [*maps, made], weights, dilations, sent, 0)


def last_kernel(layers, blocks, dilations, biases, mix, came, centre, mixed, out, made):
    map_body(layers - 1, blocks, came, centre, dilations, biases, made)

    def write(columns):
        out[...] = (mixed[...] + mix[layers] * made[:, :, columns]).astype(jnp.bfloat16)

    own_half(out.shape, write)


def beside_kernel(layer, last, halo, dilations, weights, *refs):
    mix, refs = (refs[0], refs[1:]) if last else (None, refs)
    maps, (centre, kept) = refs[: layer + 1], refs[layer + 1 :]
    _, width, inner = centre.shape
    reach = dilations[layer]

    @pl.loop(0, width, step=ROWS)
    def _(first):
        rows = pl.ds(pl.multiple_of(first, ROWS), ROWS)
        for z, plane in enumerate(tap_rows(layer, 0, maps, weights, reach, rows, halo)):
            centre[z, rows, :] = plane

    if not last:
        kept[...] = maps[-1][...].astype(jnp.bfloat16)
        return

    def write(columns):
        columns = slice(columns.start + halo, columns.stop + halo)
        kept[...] = sum(mix[j] * ref[:, :, columns].astype(jnp.float32) for j, ref in enumerate(maps))

    own_half(kept.shape, write)


def call(kernel, out_shape, scalars, arrays, scratch=(), cost=None):
    return pl.pallas_call(
        kernel,
        out_shape=out_shape,
        in_specs=[SMEM] * len(scalars) + [VMEM] * len(arrays),
        out_specs=jax.tree.map(lambda _: VMEM, out_shape),
        scratch_shapes=list(scratch),
        cost_estimate=cost,
    )(*scalars, *arrays)


def body(noisy, dilations, conv_weights, biases, mix_weights):
    layers = conv_weights.shape[0]
    depth, width, height = noisy.shape
    paired = lax.axis_size("gy") == 2
    halo = 0 if paired else height
    blocks = lax.axis_size("gx")
    assert height >= DMAX and lax.axis_size("gy") % 2 == 0 and width % ROWS == 0
    field = jax.ShapeDtypeStruct((depth, width, 2 * height), jnp.float32)
    wide = (depth, width, 2 * (height + halo))
    own = jax.ShapeDtypeStruct(noisy.shape, jnp.float32)
    route = routes(dilations, width)
    cost = pl.CostEstimate(flops=72 * depth * width * 2 * height, bytes_accessed=1 << 20, transcendentals=0)

    def beside(layer, newest, older):
        last = layer == layers - 1
        shapes = (field, own if last else jax.ShapeDtypeStruct(wide, jnp.bfloat16))

        scalars = (dilations, conv_weights, *([mix_weights] if last else []))

        def run(*operands):
            return call(
                functools.partial(beside_kernel, layer, last, halo),
                shapes,
                operands[: len(scalars)],
                operands[len(scalars) :],
                cost=cost,
            )

        return run, (*scalars, *older, newest)

    def send(layer, newest, older):
        return call(
            functools.partial(sent_kernel, layer, halo), field, (dilations, conv_weights), (*older, newest)
        )

    came = pair_gather(noisy.astype(jnp.float32))
    older = []
    if paired:
        newest, sent = call(first_kernel, (field, field), (dilations, conv_weights), (came,))
    else:
        newest = widen(jnp.concatenate([came[0], came[1]], axis=-1))
        sent = send(0, newest, older)
    for layer in range(1, layers):
        came, (centre, kept) = exchange(sent, beside(layer - 1, newest, older), route[layer - 1])
        older.append(kept)
        if paired:
            newest, sent = call(
                functools.partial(layer_kernel, layer, blocks),
                (field, field),
                (dilations, conv_weights, biases),
                (came, centre, *older),
            )
        else:
            newest = call(
                functools.partial(map_kernel, layer - 1, blocks), field, (dilations, biases), (came, centre)
            )
            newest = widen(newest)
            sent = send(layer, newest, older)
    came, (centre, mixed) = exchange(sent, beside(layers - 1, newest, older), route[layers - 1])
    return call(
        functools.partial(last_kernel, layers, blocks),
        jax.ShapeDtypeStruct(noisy.shape, jnp.bfloat16),
        (dilations, biases, mix_weights),
        (came, centre, mixed),
        scratch=[pltpu.VMEM(field.shape, jnp.float32)],
    )


def solution(mesh):
    return jax.shard_map(
        body,
        mesh=mesh,
        in_specs=(P(None, "gx", "gy"), P(), P(), P(), P()),
        out_specs=P(None, "gx", "gy"),
        check_vma=False,
    )
```

```python
import functools

import jax
import jax.numpy as jnp
from jax import lax
from jax.experimental import pallas as pl
from jax.experimental.pallas import tpu as pltpu
from jax.sharding import PartitionSpec as P

DMAX = 256
ROWS = 32
FEW = 16
CHUNK = 16
SMEM = pl.BlockSpec(memory_space=pltpu.SMEM)
VMEM = pl.BlockSpec(memory_space=pltpu.VMEM)


def pair_gather(value):
    count = lax.axis_size("gy")
    groups = None if count == 2 else [[i, i + 1] for i in range(0, count, 2)]
    return lax.all_gather(value, "gy", axis=0, axis_index_groups=groups)


def widen(field):
    count = lax.axis_size("gy")
    if count == 2:
        return field
    height = field.shape[-1] // 2
    before = lax.ppermute(field[..., height:], "gy", [(i, i + 2) for i in range(count - 2)])
    after = lax.ppermute(field[..., :height], "gy", [(i + 2, i) for i in range(count - 2)])
    return jnp.concatenate([before, field, after], axis=-1)


def outward(value, steps, flip):
    blocks, columns = lax.axis_size("gx"), lax.axis_size("gy")
    moves = []
    for k in range(blocks):
        for g in range(columns):
            target = k - steps if g % 2 == flip else k + steps
            inside = 0 <= target < blocks
            moves.append((k * columns + g, target * columns + g if inside else k * columns + (g ^ 1)))
    return lax.ppermute(value, ("gx", "gy"), moves)


def branch_counts(width):
    most = -(-DMAX // width)
    parts = width // CHUNK
    return most, parts, most * parts + most


def exchange(fields, finish, operands, route):
    width = fields[0].shape[1]
    most, parts, _ = branch_counts(width)

    def straddling(blocks, part, fields, operands):
        came = []
        for flip, field in enumerate(fields):
            near = field[:, : width - part * CHUNK]
            if blocks > 0:
                near = outward(near, blocks, flip)
            far = outward(field[:, width - (part + 1) * CHUNK :], blocks + 1, flip)
            came.append(jnp.concatenate([near, far], axis=1))
        return finish(came, *operands)

    def exact(blocks, fields, operands):
        came = []
        for flip, field in enumerate(fields):
            near = outward(field, blocks, flip)
            came.append(jnp.concatenate([near, jnp.zeros_like(near[:, :CHUNK])], axis=1))
        return finish(came, *operands)

    branches = [
        functools.partial(straddling, blocks, part) for blocks in range(most) for part in range(parts)
    ]
    branches += [functools.partial(exact, blocks) for blocks in range(1, most + 1)]
    return lax.switch(route, branches, fields, operands)


def tap_rows(layer, a, maps, weights, reach, rows, halo):
    depth, _, wide = maps[0].shape
    inner = wide - 2 * halo
    loaded = [[ref[z, rows, :].astype(jnp.float32) for z in range(depth)] for ref in maps]
    column = lax.broadcasted_iota(jnp.int32, (loaded[0][0].shape[0], inner), 1)
    sums = []
    for z in range(depth):
        total = None
        for b in (-1, 0, 1):
            part = None
            for j, planes in enumerate(loaded):
                for c in (-1, 0, 1):
                    if 0 <= z + c < depth:
                        weight = weights[layer, j, 9 * (c + 1) + 3 * (a + 1) + (b + 1)]
                        term = weight * planes[z + c]
                        part = term if part is None else part + term
            if b == 1:
                part = pltpu.roll(part, wide - reach, 1)
            elif b == -1:
                part = pltpu.roll(part, reach, 1)
            part = part[:, halo : halo + inner]
            if halo == 0 and b == 1:
                part = jnp.where(column < inner - reach, part, 0.0)
            elif halo == 0 and b == -1:
                part = jnp.where(column >= reach, part, 0.0)
            total = part if total is None else total + part
        sums.append(total)
    return sums


def reach_of(params, layer):
    return params[0, layer].astype(jnp.int32)


def bias_of(params, layer):
    return params[1, layer]


def mix_of(params, j):
    return params[2, j]


def member():
    return lax.rem(lax.axis_index("gy"), 2)


def turned_up(field, reach):
    width = field.shape[0]
    return pltpu.roll(field, lax.rem(width - lax.rem(reach, width), width), 0)


def joined(near, far, reach, width):
    row = lax.broadcasted_iota(jnp.int32, near.shape, 0)
    return jnp.where(row < width - lax.rem(reach, width), near, far)


def from_above(came, reach, blocks):
    width = came.shape[0] - CHUNK
    block = lax.axis_index("gx")
    field = joined(came[:width], came[CHUNK:], reach, width)
    row = lax.broadcasted_iota(jnp.int32, field.shape, 0)
    return jnp.where(row < (blocks - block) * width - reach, field, 0.0)


def from_below(came, reach, blocks):
    width = came.shape[0] - CHUNK
    block = lax.axis_index("gx")
    field = pltpu.roll(joined(came[:width], came[CHUNK:], reach, width), lax.rem(reach, width), 0)
    row = lax.broadcasted_iota(jnp.int32, field.shape, 0)
    return jnp.where(row >= reach - block * width, field, 0.0)


def kept_as_map(total):
    return jnp.maximum(total, 0.0).astype(jnp.bfloat16).astype(jnp.float32)


def sent_body(layer, maps, weights, params, sent, halo):
    depth, width, _ = sent.shape
    reach = reach_of(params, layer)
    side = member()

    @pl.loop(0, width, step=ROWS)
    def _(first):
        rows = pl.ds(pl.multiple_of(first, ROWS), ROWS)
        for z, plane in enumerate(tap_rows(layer, 1 - 2 * side, maps, weights, reach, rows, halo)):
            sent[z, rows, :] = plane

    @pl.when(side == 0)
    def _():
        for z in range(depth):
            sent[z] = turned_up(sent[z], reach)


def map_body(layer, blocks, came, centre, params, made):
    reach = reach_of(params, layer)
    for z in range(centre.shape[0]):
        upper = from_above(came[0, z], reach, blocks)
        lower = from_below(came[1, z], reach, blocks)
        made[z] = kept_as_map(centre[z] + upper + lower + bias_of(params, layer))


def windows_body(blocks, came, params, above, below):
    reach = reach_of(params, 0)
    height = came.shape[-1]
    for half in (0, 1):
        columns = slice(half * height, (half + 1) * height)
        for z in range(above.shape[0]):
            above[z, :, columns] = from_above(came[half, half, z], reach, blocks)
            below[z, :, columns] = from_below(came[half, 1 - half, z], reach, blocks)


def first_map_body(above, below, centre, weights, params, made, halo):
    depth, width, _ = centre.shape
    reach = reach_of(params, 0)

    @pl.loop(0, width, step=ROWS)
    def _(first):
        rows = pl.ds(pl.multiple_of(first, ROWS), ROWS)
        upper = tap_rows(0, 1, [above], weights, reach, rows, halo)
        lower = tap_rows(0, -1, [below], weights, reach, rows, halo)
        for z in range(depth):
            made[z, rows, :] = kept_as_map(centre[z, rows, :] + upper[z] + lower[z] + bias_of(params, 0))


def own_half(ref_shape, write):
    half = ref_shape[-1]
    for side in (0, 1):
        pl.when(member() == side)(functools.partial(write, slice(side * half, (side + 1) * half)))


def start_kernel(dilations, biases, mix, noisy, own, ahead, behind, packed, params):
    depth, width, _ = noisy.shape
    layers = dilations.shape[0]
    most, parts, total = branch_counts(width)
    column = lax.broadcasted_iota(jnp.int32, (1, params.shape[1]), 1)
    for row, values in enumerate((dilations, biases, mix)):
        line = jnp.zeros(column.shape, jnp.float32)
        for i in range(values.shape[0]):
            line = jnp.where(column == i, values[i].astype(jnp.float32), line)
        params[row : row + 1] = line
    code = -1
    for i in range(layers):
        reach = dilations[i]
        whole = most * parts - 1 + lax.div(reach, width)
        route = jnp.where(lax.rem(reach, width) == 0, whole, lax.div(reach - 1, CHUNK))
        code = code + (route << (i * total.bit_length()))
    packed[0] = code
    for z in range(depth):
        own[z] = noisy[z].astype(jnp.float32)
    for side, up, down in ((0, ahead, behind), (1, behind, ahead)):

        @pl.when(member() == side)
        def _():
            for z in range(depth):
                up[z] = turned_up(own[z], dilations[0])
                down[z] = own[z]


def windows_kernel(blocks, params, came, above, below):
    windows_body(blocks, came, params, above, below)


def first_map_kernel(halo, weights, params, above, below, centre, made):
    first_map_body(above, below, centre, weights, params, made, halo)


def first_layer_kernel(blocks, weights, params, came, centre, first, made, sent, above, below):
    windows_body(blocks, came, params, above, below)
    first_map_body(above, below, centre, weights, params, made, 0)
    sent_body(1, [first, made], weights, params, sent, 0)


def sent_kernel(layer, halo, weights, params, *refs):
    sent_body(layer, refs[:-1], weights, params, refs[-1], halo)


def map_kernel(layer, blocks, params, came, centre, made):
    map_body(layer, blocks, came, centre, params, made)


def layer_kernel(layer, blocks, weights, params, came, centre, *refs):
    maps, (made, sent) = refs[:layer], refs[layer:]
    map_body(layer - 1, blocks, came, centre, params, made)
    sent_body(layer, [*maps, made], weights, params, sent, 0)


def last_kernel(layers, blocks, params, came, centre, mixed, out, made):
    map_body(layers - 1, blocks, came, centre, params, made)

    def write(columns):
        out[...] = (mixed[...] + mix_of(params, layers) * made[:, :, columns]).astype(jnp.bfloat16)

    own_half(out.shape, write)


def first_beside_kernel(weights, params, pair, centre, kept, newest):
    height = pair.shape[-1]
    newest[:, :, :height] = pair[0]
    newest[:, :, height:] = pair[1]
    beside_kernel(0, False, 0, weights, params, newest, centre, kept)


def beside_kernel(layer, last, halo, weights, params, *refs):
    maps, (centre, kept) = refs[: layer + 1], refs[layer + 1 :]
    _, width, inner = centre.shape
    reach = reach_of(params, layer)

    @pl.loop(0, width, step=FEW)
    def _(first):
        rows = pl.ds(pl.multiple_of(first, FEW), FEW)
        for z, plane in enumerate(tap_rows(layer, 0, maps, weights, reach, rows, halo)):
            centre[z, rows, :] = plane

    if not last:
        kept[...] = maps[-1][...].astype(jnp.bfloat16)
        return

    def write(columns):
        columns = slice(columns.start + halo, columns.stop + halo)
        kept[...] = sum(mix_of(params, j) * ref[:, :, columns].astype(jnp.float32) for j, ref in enumerate(maps))

    own_half(kept.shape, write)


def call(kernel, out_shape, scalars, arrays, parked=0, scratch=(), cost=None, out_specs=None):
    outs = jax.tree.leaves(out_shape)
    if out_specs is None:
        out_specs = jax.tree.map(lambda _: VMEM, out_shape)
    buffers = [pltpu.VMEM(array.shape, array.dtype) for array in arrays[:parked]]
    ends = [len(scalars), len(scalars) + parked, len(scalars) + len(arrays) + len(outs)]

    def fetching(*refs):
        held = refs[ends[2] : ends[2] + parked]
        sems = refs[-1]
        copies = [
            pltpu.make_async_copy(ref, buffer, sems.at[i])
            for i, (ref, buffer) in enumerate(zip(refs[ends[0] : ends[1]], held))
        ]
        for copy in copies:
            copy.start()
        for copy in copies:
            copy.wait()
        kernel(*refs[: ends[0]], *held, *refs[ends[1] : ends[2]], *refs[ends[2] + parked : -1])

    hbm = pl.BlockSpec(memory_space=pltpu.HBM)
    return pl.pallas_call(
        fetching if parked else kernel,
        out_shape=out_shape,
        in_specs=[SMEM] * len(scalars) + [hbm] * parked + [VMEM] * (len(arrays) - parked),
        out_specs=out_specs,
        scratch_shapes=[*buffers, *scratch, *([pltpu.SemaphoreType.DMA((parked,))] if parked else [])],
        cost_estimate=cost,
    )(*scalars, *arrays)


def body(noisy, dilations, conv_weights, biases, mix_weights):
    layers = conv_weights.shape[0]
    depth, width, height = noisy.shape
    blocks, paired = lax.axis_size("gx"), lax.axis_size("gy") == 2
    halo = 0 if paired else height
    assert height >= DMAX and lax.axis_size("gy") % 2 == 0 and width % ROWS == 0 and layers > 1
    field = jax.ShapeDtypeStruct((depth, width, 2 * height), jnp.float32)
    wide = (depth, width, 2 * (height + halo))
    own_shape = jax.ShapeDtypeStruct(noisy.shape, jnp.float32)
    cost = pl.CostEstimate(flops=72 * depth * width * 2 * height, bytes_accessed=1 << 20, transcendentals=0)

    own, ahead, behind, packed, params = call(
        start_kernel,
        (
            own_shape,
            own_shape,
            own_shape,
            jax.ShapeDtypeStruct((1,), jnp.int32),
            jax.ShapeDtypeStruct((8, 128), jnp.float32),
        ),
        (dilations, biases, mix_weights),
        (noisy,),
        out_specs=(VMEM, VMEM, VMEM, SMEM, VMEM),
    )
    code = packed[0] + 1
    bits = branch_counts(width)[-1].bit_length()
    route = [(code >> (bits * layer)) & ((1 << bits) - 1) for layer in range(layers)]

    def beside(layer, weights, params, maps):
        last = layer == layers - 1
        shapes = (field, own_shape if last else jax.ShapeDtypeStruct(wide, jnp.bfloat16))
        kernel = functools.partial(beside_kernel, layer, last, halo)
        return call(kernel, shapes, (weights, params), maps, cost=cost)

    def first_finish(came, weights, params, own):
        pair = pair_gather(own)
        if paired:
            shapes = (field, jax.ShapeDtypeStruct(wide, jnp.bfloat16))
            scratch = [pltpu.VMEM(field.shape, jnp.float32)]
            found = call(first_beside_kernel, shapes, (weights, params), (pair,), scratch=scratch, cost=cost)
        else:
            found = beside(0, weights, params, [widen(jnp.concatenate([pair[0], pair[1]], axis=-1))])
        return pair_gather(jnp.stack(came)), found

    def middle_finish(layer):
        return lambda came, weights, params, *maps: (pair_gather(came[0]), beside(layer, weights, params, maps))

    def last_finish(came, weights, params, *maps):
        return pair_gather(came[0]), beside(layers - 1, weights, params, maps)

    scalars = (conv_weights, params)
    came, (centre, kept) = exchange([ahead, behind], first_finish, (*scalars, own), route[0])
    older = [kept]
    for layer in range(1, layers):
        if layer == 1 and paired:
            newest, sent = call(
                functools.partial(first_layer_kernel, blocks),
                (field, field),
                scalars,
                (came, centre, kept),
                scratch=[pltpu.VMEM(field.shape, jnp.float32)] * 2,
            )
        elif paired:
            newest, sent = call(
                functools.partial(layer_kernel, layer, blocks),
                (field, field),
                scalars,
                (came, centre, *older),
            )
        else:
            if layer == 1:
                windows = call(functools.partial(windows_kernel, blocks), (field, field), (params,), (came,))
                above, below = (widen(window) for window in windows)
                newest = call(
                    functools.partial(first_map_kernel, halo), field, scalars, (above, below, centre)
                )
            else:
                newest = call(functools.partial(map_kernel, layer - 1, blocks), field, (params,), (came, centre))
            newest = widen(newest)
            sent = call(functools.partial(sent_kernel, layer, halo), field, scalars, (*older, newest))
        operands = (*scalars, *older, newest)
        if layer == layers - 1:
            came, (centre, mixed) = exchange([sent], last_finish, operands, route[layer])
            return call(
                functools.partial(last_kernel, layers, blocks),
                jax.ShapeDtypeStruct(noisy.shape, jnp.bfloat16),
                (params,),
                (came, centre, mixed),
                scratch=[pltpu.VMEM(field.shape, jnp.float32)],
            )
        came, (centre, kept) = exchange([sent], middle_finish(layer), operands, route[layer])
        older.append(kept)


def solution(mesh):
    return jax.shard_map(
        body,
        mesh=mesh,
        in_specs=(P(None, "gx", "gy"), P(), P(), P(), P()),
        out_specs=P(None, "gx", "gy"),
        check_vma=False,
    )
```

```python
import functools

import jax
import jax.numpy as jnp
from jax import lax
from jax.experimental import pallas as pl
from jax.experimental.pallas import tpu as pltpu
from jax.sharding import PartitionSpec as P

DMAX = 256
ROWS = 32
FEW = 16
CHUNK = 16
SMEM = pl.BlockSpec(memory_space=pltpu.SMEM)
VMEM = pl.BlockSpec(memory_space=pltpu.VMEM)


def pair_gather(value):
    count = lax.axis_size("gy")
    groups = None if count == 2 else [[i, i + 1] for i in range(0, count, 2)]
    return lax.all_gather(value, "gy", axis=0, axis_index_groups=groups)


def widen(field):
    count = lax.axis_size("gy")
    if count == 2:
        return field
    height = field.shape[-1] // 2
    before = lax.ppermute(field[..., height:], "gy", [(i, i + 2) for i in range(count - 2)])
    after = lax.ppermute(field[..., :height], "gy", [(i + 2, i) for i in range(count - 2)])
    return jnp.concatenate([before, field, after], axis=-1)


def outward(value, steps, flip):
    blocks, columns = lax.axis_size("gx"), lax.axis_size("gy")
    moves = []
    for k in range(blocks):
        for g in range(columns):
            target = k - steps if g % 2 == flip else k + steps
            inside = 0 <= target < blocks
            moves.append((k * columns + g, target * columns + g if inside else k * columns + (g ^ 1)))
    return lax.ppermute(value, ("gx", "gy"), moves)


def branch_counts(width):
    most = -(-DMAX // width)
    parts = width // CHUNK
    return most, parts, most * parts + most


def exchange(fields, finish, operands, route):
    width = fields[0].shape[1]
    most, parts, _ = branch_counts(width)

    def straddling(blocks, part, fields, operands):
        came = []
        for flip, field in enumerate(fields):
            near = field[:, : width - part * CHUNK]
            if blocks > 0:
                near = outward(near, blocks, flip)
            far = outward(field[:, width - (part + 1) * CHUNK :], blocks + 1, flip)
            came.append(jnp.concatenate([near, far], axis=1))
        return finish(came, *operands)

    def exact(blocks, fields, operands):
        came = []
        for flip, field in enumerate(fields):
            near = outward(field, blocks, flip)
            came.append(jnp.concatenate([near, jnp.zeros_like(near[:, :CHUNK])], axis=1))
        return finish(came, *operands)

    branches = [
        functools.partial(straddling, blocks, part) for blocks in range(most) for part in range(parts)
    ]
    branches += [functools.partial(exact, blocks) for blocks in range(1, most + 1)]
    return lax.switch(route, branches, fields, operands)


def tap_rows(layer, a, maps, weights, reach, rows, halo):
    depth, _, wide = maps[0].shape
    inner = wide - 2 * halo
    loaded = [[ref[z, rows, :].astype(jnp.float32) for z in range(depth)] for ref in maps]
    column = lax.broadcasted_iota(jnp.int32, (loaded[0][0].shape[0], inner), 1)
    sums = []
    for z in range(depth):
        total = None
        for b in (-1, 0, 1):
            part = None
            for j, planes in enumerate(loaded):
                for c in (-1, 0, 1):
                    if 0 <= z + c < depth:
                        weight = weights[layer, j, 9 * (c + 1) + 3 * (a + 1) + (b + 1)]
                        term = weight * planes[z + c]
                        part = term if part is None else part + term
            if b == 1:
                part = pltpu.roll(part, wide - reach, 1)
            elif b == -1:
                part = pltpu.roll(part, reach, 1)
            part = part[:, halo : halo + inner]
            if halo == 0 and b == 1:
                part = jnp.where(column < inner - reach, part, 0.0)
            elif halo == 0 and b == -1:
                part = jnp.where(column >= reach, part, 0.0)
            total = part if total is None else total + part
        sums.append(total)
    return sums


def own_tap_rows(layer, a, maps, weights, reach, rows, halo):
    depth, _, wide = maps[0].shape
    height = wide // 4 if halo else wide // 2
    side = member()

    def columns_of(block):
        start = pl.multiple_of(block * height, height)
        return [[ref[z, rows, pl.ds(start, height)].astype(jnp.float32) for z in range(depth)] for ref in maps]

    def weighted(planes, b, z):
        part = None
        for j, plane in enumerate(planes):
            for c in (-1, 0, 1):
                if 0 <= z + c < depth:
                    term = weights[layer, j, 9 * (c + 1) + 3 * (a + 1) + (b + 1)] * plane[z + c]
                    part = term if part is None else part + term
        return part

    place = side + 1 if halo else side
    own = columns_of(place)
    column = lax.broadcasted_iota(jnp.int32, own[0][0].shape, 1)
    if halo:
        shifts = [(1, columns_of(place + 1)), (-1, columns_of(place - 1))]
    else:
        shifts = [(1 - 2 * side, columns_of(1 - side)), (2 * side - 1, None)]
    sums = []
    for z in range(depth):
        total = weighted(own, 0, z)
        for b, beyond in shifts:
            turn = lax.rem(height - b * reach, height)
            within = (column >= jnp.maximum(-b * reach, 0)) & (column < height - jnp.maximum(b * reach, 0))
            here = pltpu.roll(weighted(own, b, z), turn, 1)
            there = 0.0 if beyond is None else pltpu.roll(weighted(beyond, b, z), turn, 1)
            total = total + jnp.where(within, here, there)
        sums.append(total)
    return sums


def reach_of(params, layer):
    return params[0, layer].astype(jnp.int32)


def bias_of(params, layer):
    return params[1, layer]


def mix_of(params, j):
    return params[2, j]


def member():
    return lax.rem(lax.axis_index("gy"), 2)


def turned_up(field, reach):
    width = field.shape[0]
    return pltpu.roll(field, lax.rem(width - lax.rem(reach, width), width), 0)


def joined(near, far, reach, width):
    row = lax.broadcasted_iota(jnp.int32, near.shape, 0)
    return jnp.where(row < width - lax.rem(reach, width), near, far)


def from_above(came, reach, blocks):
    width = came.shape[0] - CHUNK
    block = lax.axis_index("gx")
    field = joined(came[:width], came[CHUNK:], reach, width)
    row = lax.broadcasted_iota(jnp.int32, field.shape, 0)
    return jnp.where(row < (blocks - block) * width - reach, field, 0.0)


def from_below(came, reach, blocks):
    width = came.shape[0] - CHUNK
    block = lax.axis_index("gx")
    field = pltpu.roll(joined(came[:width], came[CHUNK:], reach, width), lax.rem(reach, width), 0)
    row = lax.broadcasted_iota(jnp.int32, field.shape, 0)
    return jnp.where(row >= reach - block * width, field, 0.0)


def kept_as_map(total):
    return jnp.maximum(total, 0.0).astype(jnp.bfloat16).astype(jnp.float32)


def sent_body(layer, maps, weights, params, sent, halo):
    depth, width, _ = sent.shape
    reach = reach_of(params, layer)
    side = member()

    @pl.loop(0, width, step=ROWS)
    def _(first):
        rows = pl.ds(pl.multiple_of(first, ROWS), ROWS)
        for z, plane in enumerate(tap_rows(layer, 1 - 2 * side, maps, weights, reach, rows, halo)):
            sent[z, rows, :] = plane

    @pl.when(side == 0)
    def _():
        for z in range(depth):
            sent[z] = turned_up(sent[z], reach)


def sent_both_body(layer, maps, weights, params, ahead, behind, halo):
    depth, width, _ = ahead.shape
    reach = reach_of(params, layer)
    side = member()
    for a, field in ((1 - 2 * side, ahead), (2 * side - 1, behind)):

        @pl.loop(0, width, step=FEW)
        def _(first):
            rows = pl.ds(pl.multiple_of(first, FEW), FEW)
            for z, plane in enumerate(own_tap_rows(layer, a, maps, weights, reach, rows, halo)):
                field[z, rows, :] = plane

    for way, field in ((0, ahead), (1, behind)):

        @pl.when(side == way)
        def _():
            for z in range(depth):
                field[z] = turned_up(field[z], reach)


def map_body(layer, blocks, came, centre, params, made):
    reach = reach_of(params, layer)
    for z in range(centre.shape[0]):
        upper = from_above(came[0, z], reach, blocks)
        lower = from_below(came[1, z], reach, blocks)
        made[z] = kept_as_map(centre[z] + upper + lower + bias_of(params, layer))


def windows_body(blocks, came, params, above, below):
    reach = reach_of(params, 0)
    height = came.shape[-1]
    for half in (0, 1):
        columns = slice(half * height, (half + 1) * height)
        for z in range(above.shape[0]):
            above[z, :, columns] = from_above(came[half, half, z], reach, blocks)
            below[z, :, columns] = from_below(came[half, 1 - half, z], reach, blocks)


def first_map_body(above, below, centre, weights, params, made, halo):
    depth, width, _ = centre.shape
    reach = reach_of(params, 0)

    @pl.loop(0, width, step=ROWS)
    def _(first):
        rows = pl.ds(pl.multiple_of(first, ROWS), ROWS)
        upper = tap_rows(0, 1, [above], weights, reach, rows, halo)
        lower = tap_rows(0, -1, [below], weights, reach, rows, halo)
        for z in range(depth):
            made[z, rows, :] = kept_as_map(centre[z, rows, :] + upper[z] + lower[z] + bias_of(params, 0))


def start_kernel(dilations, biases, mix, noisy, weights, own, ahead, behind, packed, params, held):
    depth, width, _ = noisy.shape
    layers = dilations.shape[0]
    held[...] = weights[...]
    most, parts, total = branch_counts(width)
    column = lax.broadcasted_iota(jnp.int32, (1, params.shape[1]), 1)
    for row, values in enumerate((dilations, biases, mix)):
        line = jnp.zeros(column.shape, jnp.float32)
        for i in range(values.shape[0]):
            line = jnp.where(column == i, values[i].astype(jnp.float32), line)
        params[row : row + 1] = line
    code = -1
    for i in range(layers):
        reach = dilations[i]
        whole = most * parts - 1 + lax.div(reach, width)
        route = jnp.where(lax.rem(reach, width) == 0, whole, lax.div(reach - 1, CHUNK))
        code = code + (route << (i * total.bit_length()))
    packed[0] = code
    for z in range(depth):
        own[z] = noisy[z].astype(jnp.float32)
    for side, up, down in ((0, ahead, behind), (1, behind, ahead)):

        @pl.when(member() == side)
        def _():
            for z in range(depth):
                up[z] = turned_up(own[z], dilations[0])
                down[z] = own[z]


def windows_kernel(blocks, params, came, above, below):
    windows_body(blocks, came, params, above, below)


def first_map_kernel(halo, weights, params, above, below, centre, made):
    first_map_body(above, below, centre, weights, params, made, halo)


def send(layer, maps, weights, params, sent, halo):
    (sent_body if len(sent) == 1 else sent_both_body)(layer, maps, weights, params, *sent, halo)


def first_layer_kernel(blocks, weights, params, came, centre, first, made, *refs):
    sent, (above, below) = refs[:-2], refs[-2:]
    windows_body(blocks, came, params, above, below)
    first_map_body(above, below, centre, weights, params, made, 0)
    send(1, [first, made], weights, params, sent, 0)


def sent_kernel(layer, halo, weights, params, *refs):
    send(layer, refs[: layer + 1], weights, params, refs[layer + 1 :], halo)


def map_kernel(layer, blocks, params, came, centre, made):
    map_body(layer, blocks, came, centre, params, made)


def layer_kernel(layer, blocks, weights, params, came, centre, *refs):
    maps, made, sent = refs[:layer], refs[layer], refs[layer + 1 :]
    map_body(layer - 1, blocks, came, centre, params, made)
    send(layer, [*maps, made], weights, params, sent, 0)


def last_kernel(layers, blocks, params, came, centre, mixed, out):
    reach, side = reach_of(params, layers - 1), member()
    for z in range(out.shape[0]):
        upper = from_above(came[side, z], reach, blocks)
        lower = from_below(came[1 - side, z], reach, blocks)
        made = kept_as_map(centre[z] + upper + lower + bias_of(params, layers - 1))
        out[z] = (mixed[z] + mix_of(params, layers) * made).astype(jnp.bfloat16)


def first_beside_kernel(weights, params, pair, centre, kept, newest):
    height = pair.shape[-1]
    newest[:, :, :height] = pair[0]
    newest[:, :, height:] = pair[1]
    beside_kernel(0, False, 0, weights, params, newest, centre, kept)


def beside_kernel(layer, last, halo, weights, params, *refs):
    maps, (centre, kept) = refs[: layer + 1], refs[layer + 1 :]
    _, width, inner = centre.shape
    reach = reach_of(params, layer)
    taps = own_tap_rows if last else tap_rows

    @pl.loop(0, width, step=FEW)
    def _(first):
        rows = pl.ds(pl.multiple_of(first, FEW), FEW)
        for z, plane in enumerate(taps(layer, 0, maps, weights, reach, rows, halo)):
            centre[z, rows, :] = plane

    if not last:
        kept[...] = maps[-1][...].astype(jnp.bfloat16)
        return

    columns = pl.ds(pl.multiple_of(halo + member() * inner, inner), inner)
    kept[...] = sum(mix_of(params, j) * ref[:, :, columns].astype(jnp.float32) for j, ref in enumerate(maps))


def call(kernel, out_shape, scalars, arrays, scratch=(), cost=None, out_specs=None):
    return pl.pallas_call(
        kernel,
        out_shape=out_shape,
        in_specs=[SMEM] * len(scalars) + [VMEM] * len(arrays),
        out_specs=jax.tree.map(lambda _: VMEM, out_shape) if out_specs is None else out_specs,
        scratch_shapes=list(scratch),
        cost_estimate=cost,
    )(*scalars, *arrays)


def body(noisy, dilations, conv_weights, biases, mix_weights):
    layers = conv_weights.shape[0]
    depth, width, height = noisy.shape
    blocks, paired = lax.axis_size("gx"), lax.axis_size("gy") == 2
    halo = 0 if paired else height
    assert height >= DMAX and lax.axis_size("gy") % 2 == 0 and width % ROWS == 0 and layers > 1
    field = jax.ShapeDtypeStruct((depth, width, 2 * height), jnp.float32)
    wide = (depth, width, 2 * (height + halo))
    own_shape = jax.ShapeDtypeStruct(noisy.shape, jnp.float32)
    cost = pl.CostEstimate(flops=72 * depth * width * 2 * height, bytes_accessed=1 << 20, transcendentals=0)

    own, ahead, behind, packed, params, weights = call(
        start_kernel,
        (
            own_shape,
            own_shape,
            own_shape,
            pltpu.SMEM((1,), jnp.int32),
            jax.ShapeDtypeStruct((8, 128), jnp.float32),
            jax.ShapeDtypeStruct(conv_weights.shape, jnp.float32),
        ),
        (dilations, biases, mix_weights),
        (noisy, conv_weights),
        out_specs=(VMEM, VMEM, VMEM, SMEM, VMEM, VMEM),
    )
    code = packed[0] + 1
    bits = branch_counts(width)[-1].bit_length()
    route = [(code >> (bits * layer)) & ((1 << bits) - 1) for layer in range(layers)]

    def beside(layer, weights, params, maps):
        last = layer == layers - 1
        shapes = (own_shape, own_shape) if last else (field, jax.ShapeDtypeStruct(wide, jnp.bfloat16))
        kernel = functools.partial(beside_kernel, layer, last, halo)
        return call(kernel, shapes, (weights, params), maps, cost=cost)

    def first_finish(came, weights, params, own):
        pair = pair_gather(own)
        if paired:
            shapes = (field, jax.ShapeDtypeStruct(wide, jnp.bfloat16))
            scratch = [pltpu.VMEM(field.shape, jnp.float32)]
            found = call(first_beside_kernel, shapes, (weights, params), (pair,), scratch=scratch, cost=cost)
        else:
            found = beside(0, weights, params, [widen(jnp.concatenate([pair[0], pair[1]], axis=-1))])
        return pair_gather(jnp.stack(came)), found

    def middle_finish(layer):
        return lambda came, weights, params, *maps: (pair_gather(came[0]), beside(layer, weights, params, maps))

    def last_finish(came, weights, params, *maps):
        return jnp.stack(came), beside(layers - 1, weights, params, maps)

    scalars = (weights, params)
    came, (centre, kept) = exchange([ahead, behind], first_finish, (*scalars, own), route[0])
    older = [kept]
    for layer in range(1, layers):
        last = layer == layers - 1
        sent_shapes = [own_shape] * 2 if last else [field]
        if layer == 1 and paired:
            newest, *sent = call(
                functools.partial(first_layer_kernel, blocks),
                (field, *sent_shapes),
                scalars,
                (came, centre, kept),
                scratch=[pltpu.VMEM(field.shape, jnp.float32)] * 2,
            )
        elif paired:
            newest, *sent = call(
                functools.partial(layer_kernel, layer, blocks),
                (field, *sent_shapes),
                scalars,
                (came, centre, *older),
            )
        else:
            if layer == 1:
                windows = call(functools.partial(windows_kernel, blocks), (field, field), (params,), (came,))
                above, below = (widen(window) for window in windows)
                newest = call(
                    functools.partial(first_map_kernel, halo), field, scalars, (above, below, centre)
                )
            else:
                newest = call(functools.partial(map_kernel, layer - 1, blocks), field, (params,), (came, centre))
            newest = widen(newest)
            sent = call(
                functools.partial(sent_kernel, layer, halo), tuple(sent_shapes), scalars, (*older, newest)
            )
        finish = last_finish if last else middle_finish(layer)
        came, (centre, kept) = exchange(list(sent), finish, (*scalars, *older, newest), route[layer])
        older.append(kept)
    return call(
        functools.partial(last_kernel, layers, blocks),
        jax.ShapeDtypeStruct(noisy.shape, jnp.bfloat16),
        (params,),
        (came, centre, kept),
    )


def solution(mesh):
    return jax.shard_map(
        body,
        mesh=mesh,
        in_specs=(P(None, "gx", "gy"), P(), P(), P(), P()),
        out_specs=P(None, "gx", "gy"),
        check_vma=False,
    )
```

```python
import functools

import jax
import jax.numpy as jnp
from jax import lax
from jax.experimental import pallas as pl
from jax.experimental.pallas import tpu as pltpu
from jax.sharding import PartitionSpec as P

DMAX = 256
LANES = 128
ROWS = 32
FEW = 16
CHUNK = 16
SMEM = pl.BlockSpec(memory_space=pltpu.SMEM)
VMEM = pl.BlockSpec(memory_space=pltpu.VMEM)


def pair_gather(value):
    count = lax.axis_size("gy")
    groups = None if count == 2 else [[i, i + 1] for i in range(0, count, 2)]
    return lax.all_gather(value, "gy", axis=0, axis_index_groups=groups)


def widen(field):
    count = lax.axis_size("gy")
    if count == 2:
        return field
    height = field.shape[-1] // 2
    before = lax.ppermute(field[..., height:], "gy", [(i, i + 2) for i in range(count - 2)])
    after = lax.ppermute(field[..., :height], "gy", [(i + 2, i) for i in range(count - 2)])
    return jnp.concatenate([before, field, after], axis=-1)


def outward(value, steps, flip):
    blocks, columns = lax.axis_size("gx"), lax.axis_size("gy")
    moves = []
    for k in range(blocks):
        for g in range(columns):
            target = k - steps if g % 2 == flip else k + steps
            inside = 0 <= target < blocks
            moves.append((k * columns + g, target * columns + g if inside else k * columns + (g ^ 1)))
    return lax.ppermute(value, ("gx", "gy"), moves)


def branch_counts(width):
    most = -(-DMAX // width)
    parts = width // CHUNK
    return most, parts, most * parts + most


def exchange(fields, finish, operands, route):
    width = fields[0].shape[1]
    most, parts, _ = branch_counts(width)

    def straddling(blocks, part, fields, operands):
        came = []
        for flip, field in enumerate(fields):
            near = field[:, : width - part * CHUNK]
            if blocks > 0:
                near = outward(near, blocks, flip)
            far = outward(field[:, width - (part + 1) * CHUNK :], blocks + 1, flip)
            came.append(jnp.concatenate([near, far], axis=1))
        return finish(came, *operands)

    def exact(blocks, fields, operands):
        came = []
        for flip, field in enumerate(fields):
            near = outward(field, blocks, flip)
            came.append(jnp.concatenate([near, jnp.zeros_like(near[:, :CHUNK])], axis=1))
        return finish(came, *operands)

    branches = [
        functools.partial(straddling, blocks, part) for blocks in range(most) for part in range(parts)
    ]
    branches += [functools.partial(exact, blocks) for blocks in range(1, most + 1)]
    return lax.switch(route, branches, fields, operands)


def tap_rows(layer, a, maps, weights, reach, rows, halo):
    depth, _, wide = maps[0].shape
    inner = wide - 2 * halo
    loaded = [[ref[z, rows, :].astype(jnp.float32) for z in range(depth)] for ref in maps]
    column = lax.broadcasted_iota(jnp.int32, (loaded[0][0].shape[0], inner), 1)
    sums = []
    for z in range(depth):
        total = None
        for b in (-1, 0, 1):
            part = None
            for j, planes in enumerate(loaded):
                for c in (-1, 0, 1):
                    if 0 <= z + c < depth:
                        weight = weights[layer, j, 9 * (c + 1) + 3 * (a + 1) + (b + 1)]
                        term = weight * planes[z + c]
                        part = term if part is None else part + term
            if b == 1:
                part = pltpu.roll(part, wide - reach, 1)
            elif b == -1:
                part = pltpu.roll(part, reach, 1)
            part = part[:, halo : halo + inner]
            if halo == 0 and b == 1:
                part = jnp.where(column < inner - reach, part, 0.0)
            elif halo == 0 and b == -1:
                part = jnp.where(column >= reach, part, 0.0)
            total = part if total is None else total + part
        sums.append(total)
    return sums


def own_tap_rows(layer, a, maps, weights, reach, rows, halo):
    depth, _, wide = maps[0].shape
    height = wide // 4 if halo else wide // 2
    side = member()

    def columns_of(block):
        start = pl.multiple_of(block * height, height)
        return [[ref[z, rows, pl.ds(start, height)].astype(jnp.float32) for z in range(depth)] for ref in maps]

    def weighted(planes, b, z):
        part = None
        for j, plane in enumerate(planes):
            for c in (-1, 0, 1):
                if 0 <= z + c < depth:
                    term = weights[layer, j, 9 * (c + 1) + 3 * (a + 1) + (b + 1)] * plane[z + c]
                    part = term if part is None else part + term
        return part

    place = side + 1 if halo else side
    own = columns_of(place)
    column = lax.broadcasted_iota(jnp.int32, own[0][0].shape, 1)
    if halo:
        shifts = [(1, columns_of(place + 1)), (-1, columns_of(place - 1))]
    else:
        shifts = [(1 - 2 * side, columns_of(1 - side)), (2 * side - 1, None)]
    sums = []
    for z in range(depth):
        total = weighted(own, 0, z)
        for b, beyond in shifts:
            turn = lax.rem(height - b * reach, height)
            within = (column >= jnp.maximum(-b * reach, 0)) & (column < height - jnp.maximum(b * reach, 0))
            here = pltpu.roll(weighted(own, b, z), turn, 1)
            there = 0.0 if beyond is None else pltpu.roll(weighted(beyond, b, z), turn, 1)
            total = total + jnp.where(within, here, there)
        sums.append(total)
    return sums


def reach_of(params, layer):
    return params[0, layer].astype(jnp.int32)


def bias_of(params, layer):
    return params[1, layer]


def mix_of(params, j):
    return params[2, j]


def member():
    return lax.rem(lax.axis_index("gy"), 2)


def turned_up(field, reach):
    width = field.shape[0]
    return pltpu.roll(field, lax.rem(width - lax.rem(reach, width), width), 0)


def joined(near, far, reach, width):
    row = lax.broadcasted_iota(jnp.int32, near.shape, 0)
    return jnp.where(row < width - lax.rem(reach, width), near, far)


def from_above(came, reach, blocks):
    width = came.shape[0] - CHUNK
    block = lax.axis_index("gx")
    field = joined(came[:width], came[CHUNK:], reach, width)
    row = lax.broadcasted_iota(jnp.int32, field.shape, 0)
    return jnp.where(row < (blocks - block) * width - reach, field, 0.0)


def from_below(came, reach, blocks):
    width = came.shape[0] - CHUNK
    block = lax.axis_index("gx")
    field = pltpu.roll(joined(came[:width], came[CHUNK:], reach, width), lax.rem(reach, width), 0)
    row = lax.broadcasted_iota(jnp.int32, field.shape, 0)
    return jnp.where(row >= reach - block * width, field, 0.0)


def kept_as_map(total):
    return jnp.maximum(total, 0.0).astype(jnp.bfloat16).astype(jnp.float32)


def sent_body(layer, maps, weights, params, sent, halo):
    depth, width, _ = sent.shape
    reach = reach_of(params, layer)
    side = member()

    @pl.loop(0, width, step=ROWS)
    def _(first):
        rows = pl.ds(pl.multiple_of(first, ROWS), ROWS)
        for z, plane in enumerate(tap_rows(layer, 1 - 2 * side, maps, weights, reach, rows, halo)):
            sent[z, rows, :] = plane

    @pl.when(side == 0)
    def _():
        for z in range(depth):
            sent[z] = turned_up(sent[z], reach)


def sent_both_body(layer, maps, weights, params, ahead, behind, halo):
    depth, width, _ = ahead.shape
    reach = reach_of(params, layer)
    side = member()

    @pl.loop(0, width, step=FEW)
    def _(first):
        rows = pl.ds(pl.multiple_of(first, FEW), FEW)
        for a, field in ((1 - 2 * side, ahead), (2 * side - 1, behind)):
            for z, plane in enumerate(own_tap_rows(layer, a, maps, weights, reach, rows, halo)):
                field[z, rows, :] = plane

    for way, field in ((0, ahead), (1, behind)):

        @pl.when(side == way)
        def _():
            for z in range(depth):
                field[z] = turned_up(field[z], reach)


def map_body(layer, blocks, came, centre, params, made):
    reach = reach_of(params, layer)

    @pl.loop(0, centre.shape[-1], step=LANES)
    def _(first):
        columns = pl.ds(pl.multiple_of(first, LANES), LANES)
        for z in range(centre.shape[0]):
            upper = from_above(came[0, z, :, columns], reach, blocks)
            lower = from_below(came[1, z, :, columns], reach, blocks)
            made[z, :, columns] = kept_as_map(centre[z, :, columns] + upper + lower + bias_of(params, layer))


def windows_body(blocks, came, params, above, below):
    reach = reach_of(params, 0)
    height = came.shape[-1]

    @pl.loop(0, height, step=LANES)
    def _(first):
        there = pl.ds(pl.multiple_of(first, LANES), LANES)
        for half in (0, 1):
            here = pl.ds(pl.multiple_of(half * height + first, LANES), LANES)
            for z in range(above.shape[0]):
                above[z, :, here] = from_above(came[half, half, z, :, there], reach, blocks)
                below[z, :, here] = from_below(came[half, 1 - half, z, :, there], reach, blocks)


def first_map_body(above, below, centre, weights, params, made, halo):
    depth, width, _ = centre.shape
    reach = reach_of(params, 0)

    @pl.loop(0, width, step=ROWS)
    def _(first):
        rows = pl.ds(pl.multiple_of(first, ROWS), ROWS)
        upper = tap_rows(0, 1, [above], weights, reach, rows, halo)
        lower = tap_rows(0, -1, [below], weights, reach, rows, halo)
        for z in range(depth):
            made[z, rows, :] = kept_as_map(centre[z, rows, :] + upper[z] + lower[z] + bias_of(params, 0))


def start_kernel(*refs):
    arguments, (own, ahead, behind, packed, params, weights) = refs[:5], refs[5:11]
    held, sems = (*refs[11:15], weights), refs[15]
    copies = [pltpu.make_async_copy(*ends, sems.at[i]) for i, ends in enumerate(zip(arguments, held))]
    for copy in copies:
        copy.start()
    for copy in copies:
        copy.wait()
    dilations, biases, mix, noisy = held[:4]
    depth, width, _ = noisy.shape
    layers = dilations.shape[0]
    most, parts, total = branch_counts(width)
    for row, values in enumerate((dilations, biases, mix)):
        for i in range(values.shape[0]):
            params[row, i] = values[i].astype(jnp.float32)
    code = -1
    for i in range(layers):
        reach = dilations[i]
        whole = most * parts - 1 + lax.div(reach, width)
        route = jnp.where(lax.rem(reach, width) == 0, whole, lax.div(reach - 1, CHUNK))
        code = code + (route << (i * total.bit_length()))
    packed[0] = code
    for z in range(depth):
        own[z] = noisy[z].astype(jnp.float32)
    for side, up, down in ((0, ahead, behind), (1, behind, ahead)):

        @pl.when(member() == side)
        def _():
            for z in range(depth):
                up[z] = turned_up(own[z], dilations[0])
                down[z] = own[z]


def windows_kernel(blocks, params, came, above, below):
    windows_body(blocks, came, params, above, below)


def first_map_kernel(halo, weights, params, above, below, centre, made):
    first_map_body(above, below, centre, weights, params, made, halo)


def send(layer, maps, weights, params, sent, halo):
    (sent_body if len(sent) == 1 else sent_both_body)(layer, maps, weights, params, *sent, halo)


def first_layer_kernel(blocks, weights, params, came, centre, first, made, *refs):
    sent, (above, below) = refs[:-2], refs[-2:]
    windows_body(blocks, came, params, above, below)
    first_map_body(above, below, centre, weights, params, made, 0)
    send(1, [first, made], weights, params, sent, 0)


def sent_kernel(layer, halo, weights, params, *refs):
    send(layer, refs[: layer + 1], weights, params, refs[layer + 1 :], halo)


def map_kernel(layer, blocks, params, came, centre, made):
    map_body(layer, blocks, came, centre, params, made)


def layer_kernel(layer, blocks, weights, params, came, centre, *refs):
    maps, made, sent = refs[:layer], refs[layer], refs[layer + 1 :]
    map_body(layer - 1, blocks, came, centre, params, made)
    send(layer, [*maps, made], weights, params, sent, 0)


def last_kernel(layers, blocks, params, came, centre, mixed, out):
    reach, side = reach_of(params, layers - 1), member()

    @pl.loop(0, out.shape[-1], step=LANES)
    def _(first):
        columns = pl.ds(pl.multiple_of(first, LANES), LANES)
        for z in range(out.shape[0]):
            upper = from_above(came[side, z, :, columns], reach, blocks)
            lower = from_below(came[1 - side, z, :, columns], reach, blocks)
            total = centre[z, :, columns] + upper + lower + bias_of(params, layers - 1)
            mixture = mixed[z, :, columns] + mix_of(params, layers) * kept_as_map(total)
            out[z, :, columns] = mixture.astype(jnp.bfloat16)


def first_beside_kernel(weights, params, pair, centre, kept, newest):
    height = pair.shape[-1]
    newest[:, :, :height] = pair[0]
    newest[:, :, height:] = pair[1]
    beside_kernel(0, False, 0, weights, params, newest, centre, kept)


def beside_kernel(layer, last, halo, weights, params, *refs):
    maps, (centre, kept) = refs[: layer + 1], refs[layer + 1 :]
    _, width, inner = centre.shape
    reach = reach_of(params, layer)
    taps = own_tap_rows if last else tap_rows

    @pl.loop(0, width, step=FEW)
    def _(first):
        rows = pl.ds(pl.multiple_of(first, FEW), FEW)
        for z, plane in enumerate(taps(layer, 0, maps, weights, reach, rows, halo)):
            centre[z, rows, :] = plane

    if not last:
        kept[...] = maps[-1][...].astype(jnp.bfloat16)
        return

    columns = pl.ds(pl.multiple_of(halo + member() * inner, inner), inner)
    kept[...] = sum(mix_of(params, j) * ref[:, :, columns].astype(jnp.float32) for j, ref in enumerate(maps))


def call(kernel, out_shape, scalars, arrays, scratch=(), cost=None):
    return pl.pallas_call(
        kernel,
        out_shape=out_shape,
        in_specs=[SMEM] * len(scalars) + [VMEM] * len(arrays),
        out_specs=jax.tree.map(lambda _: VMEM, out_shape),
        scratch_shapes=list(scratch),
        cost_estimate=cost,
    )(*scalars, *arrays)


def body(noisy, dilations, conv_weights, biases, mix_weights):
    layers = conv_weights.shape[0]
    depth, width, height = noisy.shape
    blocks, paired = lax.axis_size("gx"), lax.axis_size("gy") == 2
    halo = 0 if paired else height
    assert height >= DMAX and lax.axis_size("gy") % 2 == 0 and width % ROWS == 0 and layers > 1
    field = jax.ShapeDtypeStruct((depth, width, 2 * height), jnp.float32)
    wide = (depth, width, 2 * (height + halo))
    own_shape = jax.ShapeDtypeStruct(noisy.shape, jnp.float32)
    cost = pl.CostEstimate(flops=72 * depth * width * 2 * height, bytes_accessed=1 << 20, transcendentals=0)

    own, ahead, behind, packed, params, weights = pl.pallas_call(
        start_kernel,
        out_shape=(
            own_shape,
            own_shape,
            own_shape,
            pltpu.SMEM((1,), jnp.int32),
            pltpu.SMEM((3, layers + 1), jnp.float32),
            pltpu.SMEM(conv_weights.shape, jnp.float32),
        ),
        in_specs=[pl.BlockSpec(memory_space=pl.ANY)] * 5,
        out_specs=(VMEM, VMEM, VMEM, SMEM, SMEM, SMEM),
        scratch_shapes=[
            *(pltpu.SMEM(value.shape, value.dtype) for value in (dilations, biases, mix_weights)),
            pltpu.VMEM(noisy.shape, noisy.dtype),
            pltpu.SemaphoreType.DMA((5,)),
        ],
    )(dilations, biases, mix_weights, noisy, conv_weights)
    code = packed[0] + 1
    bits = branch_counts(width)[-1].bit_length()
    route = [(code >> (bits * layer)) & ((1 << bits) - 1) for layer in range(layers)]

    def beside(layer, weights, params, maps):
        last = layer == layers - 1
        shapes = (own_shape, own_shape) if last else (field, jax.ShapeDtypeStruct(wide, jnp.bfloat16))
        kernel = functools.partial(beside_kernel, layer, last, halo)
        return call(kernel, shapes, (weights, params), maps, cost=cost)

    def first_finish(came, weights, params, own):
        pair = pair_gather(own)
        if paired:
            pair = pltpu.with_memory_space_constraint(pair, pltpu.VMEM)
            shapes = (field, jax.ShapeDtypeStruct(wide, jnp.bfloat16))
            scratch = [pltpu.VMEM(field.shape, jnp.float32)]
            found = call(first_beside_kernel, shapes, (weights, params), (pair,), scratch=scratch, cost=cost)
        else:
            found = beside(0, weights, params, [widen(jnp.concatenate([pair[0], pair[1]], axis=-1))])
        return pair_gather(jnp.stack(came)), found

    def middle_finish(layer):
        return lambda came, weights, params, *maps: (pair_gather(came[0]), beside(layer, weights, params, maps))

    def last_finish(came, weights, params, *maps):
        return jnp.stack(came), beside(layers - 1, weights, params, maps)

    scalars = (weights, params)
    came, (centre, kept) = exchange([ahead, behind], first_finish, (*scalars, own), route[0])
    older = [kept]
    for layer in range(1, layers):
        last = layer == layers - 1
        sent_shapes = [own_shape] * 2 if last else [field]
        if layer == 1 and paired:
            newest, *sent = call(
                functools.partial(first_layer_kernel, blocks),
                (field, *sent_shapes),
                scalars,
                (came, centre, kept),
                scratch=[pltpu.VMEM(field.shape, jnp.float32)] * 2,
            )
        elif paired:
            newest, *sent = call(
                functools.partial(layer_kernel, layer, blocks),
                (field, *sent_shapes),
                scalars,
                (came, centre, *older),
            )
        else:
            if layer == 1:
                windows = call(functools.partial(windows_kernel, blocks), (field, field), (params,), (came,))
                above, below = (widen(window) for window in windows)
                newest = call(
                    functools.partial(first_map_kernel, halo), field, scalars, (above, below, centre)
                )
            else:
                newest = call(functools.partial(map_kernel, layer - 1, blocks), field, (params,), (came, centre))
            newest = widen(newest)
            sent = call(
                functools.partial(sent_kernel, layer, halo), tuple(sent_shapes), scalars, (*older, newest)
            )
        finish = last_finish if last else middle_finish(layer)
        came, (centre, kept) = exchange(list(sent), finish, (*scalars, *older, newest), route[layer])
        older.append(kept)
    return call(
        functools.partial(last_kernel, layers, blocks),
        jax.ShapeDtypeStruct(noisy.shape, jnp.bfloat16),
        (params,),
        (came, centre, kept),
    )


def solution(mesh):
    return jax.shard_map(
        body,
        mesh=mesh,
        in_specs=(P(None, "gx", "gy"), P(), P(), P(), P()),
        out_specs=P(None, "gx", "gy"),
        check_vma=False,
    )
```

```python
import functools

import jax
import jax.numpy as jnp
from jax import lax
from jax.experimental import pallas as pl
from jax.experimental.pallas import tpu as pltpu
from jax.sharding import PartitionSpec as P

DMAX = 256
LANES = 128
ROWS = 32
SOME = 16
FEW = 8
CHUNK = 16
SMEM = pl.BlockSpec(memory_space=pltpu.SMEM)
VMEM = pl.BlockSpec(memory_space=pltpu.VMEM)


def pair_gather(value):
    count = lax.axis_size("gy")
    groups = None if count == 2 else [[i, i + 1] for i in range(0, count, 2)]
    return lax.all_gather(value, "gy", axis=0, axis_index_groups=groups)


def widen(field):
    count = lax.axis_size("gy")
    if count == 2:
        return field
    height = field.shape[-1] // 2
    before = lax.ppermute(field[..., height:], "gy", [(i, i + 2) for i in range(count - 2)])
    after = lax.ppermute(field[..., :height], "gy", [(i + 2, i) for i in range(count - 2)])
    return jnp.concatenate([before, field, after], axis=-1)


def outward(value, steps, flip):
    blocks, columns = lax.axis_size("gx"), lax.axis_size("gy")
    moves = []
    for k in range(blocks):
        for g in range(columns):
            target = k - steps if g % 2 == flip else k + steps
            inside = 0 <= target < blocks
            moves.append((k * columns + g, target * columns + g if inside else k * columns + (g ^ 1)))
    return lax.ppermute(value, ("gx", "gy"), moves)


def branch_counts(width):
    most = -(-DMAX // width)
    parts = width // CHUNK
    return most, parts, most * parts + most


def exchange(fields, finish, operands, route, last):
    width = fields[0].shape[1]
    most, parts, _ = branch_counts(width)

    def straddling(blocks, part, fields, operands):
        came = []
        for flip, field in enumerate(fields):
            near = field[:, : width - part * CHUNK]
            if blocks > 0:
                near = outward(near, blocks, flip)
            far = outward(field[:, width - (part + 1) * CHUNK :], blocks + 1, flip)
            came += [near, far]
        if last and part in (0, parts - 1):
            came = [jnp.concatenate(came[i : i + 2], axis=1) for i in range(0, len(came), 2)]
            came = lax.optimization_barrier(came)
        return finish(jnp.concatenate(came, axis=1), *operands)

    def exact(blocks, fields, operands):
        came = []
        for flip, field in enumerate(fields):
            near = outward(field, blocks, flip)
            came += [near, jnp.zeros_like(near[:, :CHUNK])]
        return finish(jnp.concatenate(came, axis=1), *operands)

    branches = [
        functools.partial(straddling, blocks, part) for blocks in range(most) for part in range(parts)
    ]
    branches += [functools.partial(exact, blocks) for blocks in range(1, most + 1)]
    return lax.switch(route, branches, fields, operands)


def tap_rows(layer, a, maps, weights, reach, rows, halo):
    depth, _, wide = maps[0].shape
    inner = wide - 2 * halo
    loaded = [[ref[z, rows, :].astype(jnp.float32) for z in range(depth)] for ref in maps]
    column = lax.broadcasted_iota(jnp.int32, (loaded[0][0].shape[0], inner), 1)
    sums = []
    for z in range(depth):
        total = None
        for b in (-1, 0, 1):
            part = None
            for j, planes in enumerate(loaded):
                for c in (-1, 0, 1):
                    if 0 <= z + c < depth:
                        weight = weights[layer, j, 9 * (c + 1) + 3 * (a + 1) + (b + 1)]
                        term = weight * planes[z + c]
                        part = term if part is None else part + term
            if b == 1:
                part = pltpu.roll(part, wide - reach, 1)
            elif b == -1:
                part = pltpu.roll(part, reach, 1)
            part = part[:, halo : halo + inner]
            if halo == 0 and b == 1:
                part = jnp.where(column < inner - reach, part, 0.0)
            elif halo == 0 and b == -1:
                part = jnp.where(column >= reach, part, 0.0)
            total = part if total is None else total + part
        sums.append(total)
    return sums


def own_tap_rows(layer, a, maps, weights, reach, rows, halo):
    depth, _, wide = maps[0].shape
    height = wide // 4 if halo else wide // 2
    side = member()

    def columns_of(block):
        start = pl.multiple_of(block * height, height)
        return [[ref[z, rows, pl.ds(start, height)].astype(jnp.float32) for z in range(depth)] for ref in maps]

    def weighted(planes, b, z):
        part = None
        for j, plane in enumerate(planes):
            for c in (-1, 0, 1):
                if 0 <= z + c < depth:
                    term = weights[layer, j, 9 * (c + 1) + 3 * (a + 1) + (b + 1)] * plane[z + c]
                    part = term if part is None else part + term
        return part

    place = side + 1 if halo else side
    own = columns_of(place)
    column = lax.broadcasted_iota(jnp.int32, own[0][0].shape, 1)
    if halo:
        shifts = [(1, columns_of(place + 1)), (-1, columns_of(place - 1))]
    else:
        shifts = [(1 - 2 * side, columns_of(1 - side)), (2 * side - 1, None)]
    sums = []
    for z in range(depth):
        total = weighted(own, 0, z)
        for b, beyond in shifts:
            turn = lax.rem(height - b * reach, height)
            within = (column >= jnp.maximum(-b * reach, 0)) & (column < height - jnp.maximum(b * reach, 0))
            here = pltpu.roll(weighted(own, b, z), turn, 1)
            there = 0.0 if beyond is None else pltpu.roll(weighted(beyond, b, z), turn, 1)
            total = total + jnp.where(within, here, there)
        sums.append(total)
    return sums


def reach_of(params, layer):
    return params[0, layer].astype(jnp.int32)


def bias_of(params, layer):
    return params[1, layer]


def mix_of(params, j):
    return params[2, j]


def member():
    return lax.rem(lax.axis_index("gy"), 2)


def turned_up(field, reach):
    width = field.shape[0]
    return pltpu.roll(field, lax.rem(width - lax.rem(reach, width), width), 0)


def joined(near, far, reach, width):
    row = lax.broadcasted_iota(jnp.int32, near.shape, 0)
    return jnp.where(row < width - lax.rem(reach, width), near, far)


def field_of(came, which, z, columns):
    rows = came.shape[1] // 2
    return came[z, pl.ds(pl.multiple_of(which * rows, CHUNK), rows), columns]


def from_above(came, reach, blocks):
    width = came.shape[0] - CHUNK
    block = lax.axis_index("gx")
    field = joined(came[:width], came[CHUNK:], reach, width)
    row = lax.broadcasted_iota(jnp.int32, field.shape, 0)
    return jnp.where(row < (blocks - block) * width - reach, field, 0.0)


def from_below(came, reach, blocks):
    width = came.shape[0] - CHUNK
    block = lax.axis_index("gx")
    field = pltpu.roll(joined(came[:width], came[CHUNK:], reach, width), lax.rem(reach, width), 0)
    row = lax.broadcasted_iota(jnp.int32, field.shape, 0)
    return jnp.where(row >= reach - block * width, field, 0.0)


def kept_as_map(total):
    return jnp.maximum(total, 0.0).astype(jnp.bfloat16).astype(jnp.float32)


def sent_body(layer, maps, weights, params, sent, halo):
    depth, width, _ = sent.shape
    reach = reach_of(params, layer)
    side = member()

    @pl.loop(0, width, step=ROWS)
    def _(first):
        rows = pl.ds(pl.multiple_of(first, ROWS), ROWS)
        for z, plane in enumerate(tap_rows(layer, 1 - 2 * side, maps, weights, reach, rows, halo)):
            sent[z, rows, :] = plane

    @pl.when(side == 0)
    def _():
        for z in range(depth):
            sent[z] = turned_up(sent[z], reach)


def sent_both_body(layer, maps, weights, params, ahead, behind, halo):
    depth, width, _ = ahead.shape
    reach = reach_of(params, layer)
    side = member()

    @pl.loop(0, width, step=SOME)
    def _(first):
        rows = pl.ds(pl.multiple_of(first, SOME), SOME)
        for a, field in ((1 - 2 * side, ahead), (2 * side - 1, behind)):
            for z, plane in enumerate(own_tap_rows(layer, a, maps, weights, reach, rows, halo)):
                field[z, rows, :] = plane

    for way, field in ((0, ahead), (1, behind)):

        @pl.when(side == way)
        def _():
            for z in range(depth):
                field[z] = turned_up(field[z], reach)


def map_body(layer, blocks, came, centre, params, made):
    reach = reach_of(params, layer)

    @pl.loop(0, centre.shape[-1], step=LANES)
    def _(first):
        columns = pl.ds(pl.multiple_of(first, LANES), LANES)
        for z in range(centre.shape[0]):
            upper = from_above(came[0, z, :, columns], reach, blocks)
            lower = from_below(came[1, z, :, columns], reach, blocks)
            made[z, :, columns] = kept_as_map(centre[z, :, columns] + upper + lower + bias_of(params, layer))


def windows_body(blocks, came, params, above, below):
    reach = reach_of(params, 0)
    height = came.shape[-1]

    @pl.loop(0, height, step=LANES)
    def _(first):
        there = pl.ds(pl.multiple_of(first, LANES), LANES)
        for half in (0, 1):
            here = pl.ds(pl.multiple_of(half * height + first, LANES), LANES)
            for z in range(above.shape[0]):
                above[z, :, here] = from_above(field_of(came.at[half], half, z, there), reach, blocks)
                below[z, :, here] = from_below(field_of(came.at[half], 1 - half, z, there), reach, blocks)


def first_map_body(above, below, centre, weights, params, made, halo):
    depth, width, _ = centre.shape
    reach = reach_of(params, 0)

    @pl.loop(0, width, step=ROWS)
    def _(first):
        rows = pl.ds(pl.multiple_of(first, ROWS), ROWS)
        upper = tap_rows(0, 1, [above], weights, reach, rows, halo)
        lower = tap_rows(0, -1, [below], weights, reach, rows, halo)
        for z in range(depth):
            made[z, rows, :] = kept_as_map(centre[z, rows, :] + upper[z] + lower[z] + bias_of(params, 0))


def start_kernel(*refs):
    arguments, (own, ahead, behind, packed, params, weights) = refs[:5], refs[5:11]
    held, sems = (*refs[11:15], weights), refs[15]
    copies = [pltpu.make_async_copy(*ends, sems.at[i]) for i, ends in enumerate(zip(arguments, held))]
    for copy in copies:
        copy.start()
    for copy in copies:
        copy.wait()
    dilations, biases, mix, noisy = held[:4]
    depth, width, _ = noisy.shape
    layers = dilations.shape[0]
    most, parts, total = branch_counts(width)
    for row, values in enumerate((dilations, biases, mix)):
        for i in range(values.shape[0]):
            params[row, i] = values[i].astype(jnp.float32)
    code = -1
    for i in range(layers):
        reach = dilations[i]
        whole = most * parts - 1 + lax.div(reach, width)
        route = jnp.where(lax.rem(reach, width) == 0, whole, lax.div(reach - 1, CHUNK))
        code = code + (route << (i * total.bit_length()))
    packed[0] = code
    for z in range(depth):
        own[z] = noisy[z].astype(jnp.float32)
    for side, up, down in ((0, ahead, behind), (1, behind, ahead)):

        @pl.when(member() == side)
        def _():
            for z in range(depth):
                up[z] = turned_up(own[z], dilations[0])
                down[z] = own[z]


def windows_kernel(blocks, params, came, above, below):
    windows_body(blocks, came, params, above, below)


def first_map_kernel(halo, weights, params, above, below, centre, made):
    first_map_body(above, below, centre, weights, params, made, halo)


def send(layer, maps, weights, params, sent, halo):
    (sent_body if len(sent) == 1 else sent_both_body)(layer, maps, weights, params, *sent, halo)


def first_layer_kernel(blocks, weights, params, came, centre, first, made, *refs):
    sent, (above, below) = refs[:-2], refs[-2:]
    windows_body(blocks, came, params, above, below)
    first_map_body(above, below, centre, weights, params, made, 0)
    send(1, [first, made], weights, params, sent, 0)


def sent_kernel(layer, halo, weights, params, *refs):
    send(layer, refs[: layer + 1], weights, params, refs[layer + 1 :], halo)


def map_kernel(layer, blocks, params, came, centre, made):
    map_body(layer, blocks, came, centre, params, made)


def layer_kernel(layer, blocks, weights, params, came, centre, *refs):
    maps, made, sent = refs[:layer], refs[layer], refs[layer + 1 :]
    map_body(layer - 1, blocks, came, centre, params, made)
    send(layer, [*maps, made], weights, params, sent, 0)


def last_kernel(layers, blocks, params, came, centre, mixed, out):
    reach, side = reach_of(params, layers - 1), member()

    @pl.loop(0, out.shape[-1], step=LANES)
    def _(first):
        columns = pl.ds(pl.multiple_of(first, LANES), LANES)
        for z in range(out.shape[0]):
            upper = from_above(field_of(came, side, z, columns), reach, blocks)
            lower = from_below(field_of(came, 1 - side, z, columns), reach, blocks)
            total = centre[z, :, columns] + upper + lower + bias_of(params, layers - 1)
            mixture = mixed[z, :, columns] + mix_of(params, layers) * kept_as_map(total)
            out[z, :, columns] = mixture.astype(jnp.bfloat16)


def first_beside_kernel(weights, params, pair, centre, kept, newest):
    height = pair.shape[-1]
    newest[:, :, :height] = pair[0]
    newest[:, :, height:] = pair[1]
    beside_kernel(0, False, 0, weights, params, newest, centre, kept)


def beside_kernel(layer, last, halo, weights, params, *refs):
    maps, (centre, kept) = refs[: layer + 1], refs[layer + 1 :]
    _, width, inner = centre.shape
    reach = reach_of(params, layer)
    taps = own_tap_rows if last else tap_rows

    @pl.loop(0, width, step=FEW)
    def _(first):
        rows = pl.ds(pl.multiple_of(first, FEW), FEW)
        for z, plane in enumerate(taps(layer, 0, maps, weights, reach, rows, halo)):
            centre[z, rows, :] = plane

    if not last:
        kept[...] = maps[-1][...].astype(jnp.bfloat16)
        return

    columns = pl.ds(pl.multiple_of(halo + member() * inner, inner), inner)
    kept[...] = sum(mix_of(params, j) * ref[:, :, columns].astype(jnp.float32) for j, ref in enumerate(maps))


def call(kernel, out_shape, scalars, arrays, scratch=(), cost=None):
    return pl.pallas_call(
        kernel,
        out_shape=out_shape,
        in_specs=[SMEM] * len(scalars) + [VMEM] * len(arrays),
        out_specs=jax.tree.map(lambda _: VMEM, out_shape),
        scratch_shapes=list(scratch),
        cost_estimate=cost,
    )(*scalars, *arrays)


def body(noisy, dilations, conv_weights, biases, mix_weights):
    layers = conv_weights.shape[0]
    depth, width, height = noisy.shape
    blocks, paired = lax.axis_size("gx"), lax.axis_size("gy") == 2
    halo = 0 if paired else height
    assert height >= DMAX and lax.axis_size("gy") % 2 == 0 and width % ROWS == 0 and layers > 1
    field = jax.ShapeDtypeStruct((depth, width, 2 * height), jnp.float32)
    wide = (depth, width, 2 * (height + halo))
    own_shape = jax.ShapeDtypeStruct(noisy.shape, jnp.float32)
    cost = pl.CostEstimate(flops=72 * depth * width * 2 * height, bytes_accessed=1 << 20, transcendentals=0)

    own, ahead, behind, packed, params, weights = pl.pallas_call(
        start_kernel,
        out_shape=(
            own_shape,
            own_shape,
            own_shape,
            pltpu.SMEM((1,), jnp.int32),
            pltpu.SMEM((3, layers + 1), jnp.float32),
            pltpu.SMEM(conv_weights.shape, jnp.float32),
        ),
        in_specs=[pl.BlockSpec(memory_space=pl.ANY)] * 5,
        out_specs=(VMEM, VMEM, VMEM, SMEM, SMEM, SMEM),
        scratch_shapes=[
            *(pltpu.SMEM(value.shape, value.dtype) for value in (dilations, biases, mix_weights)),
            pltpu.VMEM(noisy.shape, noisy.dtype),
            pltpu.SemaphoreType.DMA((5,)),
        ],
    )(dilations, biases, mix_weights, noisy, conv_weights)
    code = packed[0] + 1
    bits = branch_counts(width)[-1].bit_length()
    route = [(code >> (bits * layer)) & ((1 << bits) - 1) for layer in range(layers)]

    def beside(layer, weights, params, maps):
        last = layer == layers - 1
        shapes = (own_shape, own_shape) if last else (field, jax.ShapeDtypeStruct(wide, jnp.bfloat16))
        kernel = functools.partial(beside_kernel, layer, last, halo)
        return call(kernel, shapes, (weights, params), maps, cost=cost)

    def first_finish(came, weights, params, own):
        pair = pair_gather(own)
        if paired:
            pair = pltpu.with_memory_space_constraint(pair, pltpu.VMEM)
            shapes = (field, jax.ShapeDtypeStruct(wide, jnp.bfloat16))
            scratch = [pltpu.VMEM(field.shape, jnp.float32)]
            found = call(first_beside_kernel, shapes, (weights, params), (pair,), scratch=scratch, cost=cost)
        else:
            found = beside(0, weights, params, [widen(jnp.concatenate([pair[0], pair[1]], axis=-1))])
        return pair_gather(came), found

    def middle_finish(layer):
        return lambda came, weights, params, *maps: (pair_gather(came), beside(layer, weights, params, maps))

    def last_finish(came, weights, params, *maps):
        return came, beside(layers - 1, weights, params, maps)

    scalars = (weights, params)
    came, (centre, kept) = exchange([ahead, behind], first_finish, (*scalars, own), route[0], False)
    older = [kept]
    for layer in range(1, layers):
        last = layer == layers - 1
        sent_shapes = [own_shape] * 2 if last else [field]
        if layer == 1 and paired:
            newest, *sent = call(
                functools.partial(first_layer_kernel, blocks),
                (field, *sent_shapes),
                scalars,
                (came, centre, kept),
                scratch=[pltpu.VMEM(field.shape, jnp.float32)] * 2,
            )
        elif paired:
            newest, *sent = call(
                functools.partial(layer_kernel, layer, blocks),
                (field, *sent_shapes),
                scalars,
                (came, centre, *older),
            )
        else:
            if layer == 1:
                windows = call(functools.partial(windows_kernel, blocks), (field, field), (params,), (came,))
                above, below = (widen(window) for window in windows)
                newest = call(
                    functools.partial(first_map_kernel, halo), field, scalars, (above, below, centre)
                )
            else:
                newest = call(functools.partial(map_kernel, layer - 1, blocks), field, (params,), (came, centre))
            newest = widen(newest)
            sent = call(
                functools.partial(sent_kernel, layer, halo), tuple(sent_shapes), scalars, (*older, newest)
            )
        finish = last_finish if last else middle_finish(layer)
        came, (centre, kept) = exchange(
            list(sent), finish, (*scalars, *older, newest), route[layer], last
        )
        older.append(kept)
    return call(
        functools.partial(last_kernel, layers, blocks),
        jax.ShapeDtypeStruct(noisy.shape, jnp.bfloat16),
        (params,),
        (came, centre, kept),
    )


def solution(mesh):
    return jax.shard_map(
        body,
        mesh=mesh,
        in_specs=(P(None, "gx", "gy"), P(), P(), P(), P()),
        out_specs=P(None, "gx", "gy"),
        check_vma=False,
    )
```

```python
import functools

import jax
import jax.numpy as jnp
from jax import lax
from jax.experimental import pallas as pl
from jax.experimental.pallas import tpu as pltpu
from jax.sharding import PartitionSpec as P

DMAX = 256
LANES = 128
ROWS = 64
SOME = 32
FEW = 8
CHUNK = 16
SMEM = pl.BlockSpec(memory_space=pltpu.SMEM)
VMEM = pl.BlockSpec(memory_space=pltpu.VMEM)


def pair_gather(value):
    count = lax.axis_size("gy")
    groups = None if count == 2 else [[i, i + 1] for i in range(0, count, 2)]
    return lax.all_gather(value, "gy", axis=0, axis_index_groups=groups)


def widen(field):
    count = lax.axis_size("gy")
    if count == 2:
        return field
    height = field.shape[-1] // 2
    before = lax.ppermute(field[..., height:], "gy", [(i, i + 2) for i in range(count - 2)])
    after = lax.ppermute(field[..., :height], "gy", [(i + 2, i) for i in range(count - 2)])
    return jnp.concatenate([before, field, after], axis=-1)


def outward(value, steps, flip):
    blocks, columns = lax.axis_size("gx"), lax.axis_size("gy")
    moves = []
    for k in range(blocks):
        for g in range(columns):
            target = k - steps if g % 2 == flip else k + steps
            inside = 0 <= target < blocks
            moves.append((k * columns + g, target * columns + g if inside else k * columns + (g ^ 1)))
    return lax.ppermute(value, ("gx", "gy"), moves)


def branch_counts(width):
    most = -(-DMAX // width)
    parts = width // CHUNK
    return most, parts, most * parts + most


def exchange(fields, finish, operands, route, last):
    width = fields[0].shape[1]
    most, parts, _ = branch_counts(width)

    def straddling(blocks, part, fields, operands):
        came = []
        for flip, field in enumerate(fields):
            near = field[:, : width - part * CHUNK]
            if blocks > 0:
                near = outward(near, blocks, flip)
            far = outward(field[:, width - (part + 1) * CHUNK :], blocks + 1, flip)
            came += [near, far]
        if last and part in (0, parts - 1):
            came = [jnp.concatenate(came[i : i + 2], axis=1) for i in range(0, len(came), 2)]
            came = lax.optimization_barrier(came)
        return finish(jnp.concatenate(came, axis=1), *operands)

    def exact(blocks, fields, operands):
        came = []
        for flip, field in enumerate(fields):
            near = outward(field, blocks, flip)
            came += [near, jnp.zeros_like(near[:, :CHUNK])]
        return finish(jnp.concatenate(came, axis=1), *operands)

    branches = [
        functools.partial(straddling, blocks, part) for blocks in range(most) for part in range(parts)
    ]
    branches += [functools.partial(exact, blocks) for blocks in range(1, most + 1)]
    return lax.switch(route, branches, fields, operands)


def tap_rows(layer, a, maps, weights, reach, rows, halo):
    depth, _, wide = maps[0].shape
    inner = wide - 2 * halo
    loaded = [[ref[z, rows, :].astype(jnp.float32) for z in range(depth)] for ref in maps]
    column = lax.broadcasted_iota(jnp.int32, (loaded[0][0].shape[0], inner), 1)
    sums = []
    for z in range(depth):
        total = None
        for b in (-1, 0, 1):
            part = None
            for j, planes in enumerate(loaded):
                for c in (-1, 0, 1):
                    if 0 <= z + c < depth:
                        weight = weights[layer, j, 9 * (c + 1) + 3 * (a + 1) + (b + 1)]
                        term = weight * planes[z + c]
                        part = term if part is None else part + term
            if b == 1:
                part = pltpu.roll(part, wide - reach, 1)
            elif b == -1:
                part = pltpu.roll(part, reach, 1)
            part = part[:, halo : halo + inner]
            if halo == 0 and b == 1:
                part = jnp.where(column < inner - reach, part, 0.0)
            elif halo == 0 and b == -1:
                part = jnp.where(column >= reach, part, 0.0)
            total = part if total is None else total + part
        sums.append(total)
    return sums


def own_tap_rows(layer, a, maps, weights, reach, rows, halo):
    depth, _, wide = maps[0].shape
    height = wide // 4 if halo else wide // 2
    side = member()

    def columns_of(block):
        start = pl.multiple_of(block * height, height)
        return [[ref[z, rows, pl.ds(start, height)].astype(jnp.float32) for z in range(depth)] for ref in maps]

    def weighted(planes, b, z):
        part = None
        for j, plane in enumerate(planes):
            for c in (-1, 0, 1):
                if 0 <= z + c < depth:
                    term = weights[layer, j, 9 * (c + 1) + 3 * (a + 1) + (b + 1)] * plane[z + c]
                    part = term if part is None else part + term
        return part

    place = side + 1 if halo else side
    own = columns_of(place)
    column = lax.broadcasted_iota(jnp.int32, own[0][0].shape, 1)
    if halo:
        shifts = [(1, columns_of(place + 1)), (-1, columns_of(place - 1))]
    else:
        shifts = [(1 - 2 * side, columns_of(1 - side)), (2 * side - 1, None)]
    sums = []
    for z in range(depth):
        total = weighted(own, 0, z)
        for b, beyond in shifts:
            turn = lax.rem(height - b * reach, height)
            within = (column >= jnp.maximum(-b * reach, 0)) & (column < height - jnp.maximum(b * reach, 0))
            here = pltpu.roll(weighted(own, b, z), turn, 1)
            there = 0.0 if beyond is None else pltpu.roll(weighted(beyond, b, z), turn, 1)
            total = total + jnp.where(within, here, there)
        sums.append(total)
    return sums


def reach_of(params, layer):
    return params[0, layer].astype(jnp.int32)


def bias_of(params, layer):
    return params[1, layer]


def mix_of(params, j):
    return params[2, j]


def member():
    return lax.rem(lax.axis_index("gy"), 2)


def turned_up(field, reach):
    width = field.shape[0]
    return pltpu.roll(field, lax.rem(width - lax.rem(reach, width), width), 0)


def joined(near, far, reach, width):
    row = lax.broadcasted_iota(jnp.int32, near.shape, 0)
    return jnp.where(row < width - lax.rem(reach, width), near, far)


def field_of(came, which, z, columns):
    rows = came.shape[1] // 2
    return came[z, pl.ds(pl.multiple_of(which * rows, CHUNK), rows), columns]


def from_above(came, reach, blocks):
    width = came.shape[0] - CHUNK
    block = lax.axis_index("gx")
    field = joined(came[:width], came[CHUNK:], reach, width)
    row = lax.broadcasted_iota(jnp.int32, field.shape, 0)
    return jnp.where(row < (blocks - block) * width - reach, field, 0.0)


def from_below(came, reach, blocks):
    width = came.shape[0] - CHUNK
    block = lax.axis_index("gx")
    field = pltpu.roll(joined(came[:width], came[CHUNK:], reach, width), lax.rem(reach, width), 0)
    row = lax.broadcasted_iota(jnp.int32, field.shape, 0)
    return jnp.where(row >= reach - block * width, field, 0.0)


def kept_as_map(total):
    return jnp.maximum(total, 0.0).astype(jnp.bfloat16).astype(jnp.float32)


def sent_body(layer, maps, weights, params, sent, halo):
    depth, width, _ = sent.shape
    reach = reach_of(params, layer)
    side = member()

    @pl.loop(0, width, step=ROWS)
    def _(first):
        rows = pl.ds(pl.multiple_of(first, ROWS), ROWS)
        for z, plane in enumerate(tap_rows(layer, 1 - 2 * side, maps, weights, reach, rows, halo)):
            sent[z, rows, :] = plane

    @pl.when(side == 0)
    def _():
        for z in range(depth):
            sent[z] = turned_up(sent[z], reach)


def sent_both_body(layer, maps, weights, params, ahead, behind, halo):
    depth, width, _ = ahead.shape
    reach = reach_of(params, layer)
    side = member()

    @pl.loop(0, width, step=SOME)
    def _(first):
        rows = pl.ds(pl.multiple_of(first, SOME), SOME)
        for a, field in ((1 - 2 * side, ahead), (2 * side - 1, behind)):
            for z, plane in enumerate(own_tap_rows(layer, a, maps, weights, reach, rows, halo)):
                field[z, rows, :] = plane

    for way, field in ((0, ahead), (1, behind)):

        @pl.when(side == way)
        def _():
            for z in range(depth):
                field[z] = turned_up(field[z], reach)


def map_body(layer, blocks, came, centre, params, made):
    reach = reach_of(params, layer)

    @pl.loop(0, centre.shape[-1], step=LANES)
    def _(first):
        columns = pl.ds(pl.multiple_of(first, LANES), LANES)
        for z in range(centre.shape[0]):
            upper = from_above(came[0, z, :, columns], reach, blocks)
            lower = from_below(came[1, z, :, columns], reach, blocks)
            made[z, :, columns] = kept_as_map(centre[z, :, columns] + upper + lower + bias_of(params, layer))


def windows_body(blocks, came, params, above, below):
    reach = reach_of(params, 0)
    height = came.shape[-1]

    @pl.loop(0, height, step=LANES)
    def _(first):
        there = pl.ds(pl.multiple_of(first, LANES), LANES)
        for half in (0, 1):
            here = pl.ds(pl.multiple_of(half * height + first, LANES), LANES)
            for z in range(above.shape[0]):
                above[z, :, here] = from_above(field_of(came.at[half], half, z, there), reach, blocks)
                below[z, :, here] = from_below(field_of(came.at[half], 1 - half, z, there), reach, blocks)


def first_map_body(above, below, centre, weights, params, made, halo):
    depth, width, _ = centre.shape
    reach = reach_of(params, 0)

    @pl.loop(0, width, step=ROWS)
    def _(first):
        rows = pl.ds(pl.multiple_of(first, ROWS), ROWS)
        upper = tap_rows(0, 1, [above], weights, reach, rows, halo)
        lower = tap_rows(0, -1, [below], weights, reach, rows, halo)
        for z in range(depth):
            made[z, rows, :] = kept_as_map(centre[z, rows, :] + upper[z] + lower[z] + bias_of(params, 0))


def start_kernel(*refs):
    arguments, (own, ahead, behind, packed, params, weights) = refs[:5], refs[5:11]
    held, sems = (*refs[11:15], weights), refs[15]
    copies = [pltpu.make_async_copy(*ends, sems.at[i]) for i, ends in enumerate(zip(arguments, held))]
    for copy in copies:
        copy.start()
    for copy in copies:
        copy.wait()
    dilations, biases, mix, noisy = held[:4]
    depth, width, _ = noisy.shape
    layers = dilations.shape[0]
    most, parts, total = branch_counts(width)
    for row, values in enumerate((dilations, biases, mix)):
        for i in range(values.shape[0]):
            params[row, i] = values[i].astype(jnp.float32)
    code = -1
    for i in range(layers):
        reach = dilations[i]
        whole = most * parts - 1 + lax.div(reach, width)
        route = jnp.where(lax.rem(reach, width) == 0, whole, lax.div(reach - 1, CHUNK))
        code = code + (route << (i * total.bit_length()))
    packed[0] = code
    for z in range(depth):
        own[z] = noisy[z].astype(jnp.float32)
    for side, up, down in ((0, ahead, behind), (1, behind, ahead)):

        @pl.when(member() == side)
        def _():
            for z in range(depth):
                up[z] = turned_up(own[z], dilations[0])
                down[z] = own[z]


def windows_kernel(blocks, params, came, above, below):
    windows_body(blocks, came, params, above, below)


def first_map_kernel(halo, weights, params, above, below, centre, made):
    first_map_body(above, below, centre, weights, params, made, halo)


def send(layer, maps, weights, params, sent, halo):
    (sent_body if len(sent) == 1 else sent_both_body)(layer, maps, weights, params, *sent, halo)


def first_layer_kernel(blocks, weights, params, came, centre, first, made, *refs):
    sent, (above, below) = refs[:-2], refs[-2:]
    windows_body(blocks, came, params, above, below)
    first_map_body(above, below, centre, weights, params, made, 0)
    send(1, [first, made], weights, params, sent, 0)


def sent_kernel(layer, halo, weights, params, *refs):
    send(layer, refs[: layer + 1], weights, params, refs[layer + 1 :], halo)


def map_kernel(layer, blocks, params, came, centre, made):
    map_body(layer, blocks, came, centre, params, made)


def layer_kernel(layer, blocks, weights, params, came, centre, *refs):
    maps, made, sent = refs[:layer], refs[layer], refs[layer + 1 :]
    map_body(layer - 1, blocks, came, centre, params, made)
    send(layer, [*maps, made], weights, params, sent, 0)


def last_kernel(layers, blocks, params, came, centre, mixed, out):
    reach, side = reach_of(params, layers - 1), member()

    @pl.loop(0, out.shape[-1], step=LANES)
    def _(first):
        columns = pl.ds(pl.multiple_of(first, LANES), LANES)
        for z in range(out.shape[0]):
            upper = from_above(field_of(came, side, z, columns), reach, blocks)
            lower = from_below(field_of(came, 1 - side, z, columns), reach, blocks)
            total = centre[z, :, columns] + upper + lower + bias_of(params, layers - 1)
            mixture = mixed[z, :, columns] + mix_of(params, layers) * kept_as_map(total)
            out[z, :, columns] = mixture.astype(jnp.bfloat16)


def first_beside_kernel(weights, params, pair, centre, kept, newest):
    height = pair.shape[-1]
    newest[:, :, :height] = pair[0]
    newest[:, :, height:] = pair[1]
    beside_kernel(0, False, 0, weights, params, newest, centre, kept)


def beside_kernel(layer, last, halo, weights, params, *refs):
    maps, (centre, kept) = refs[: layer + 1], refs[layer + 1 :]
    _, width, inner = centre.shape
    reach = reach_of(params, layer)
    taps = own_tap_rows if last else tap_rows

    @pl.loop(0, width, step=FEW)
    def _(first):
        rows = pl.ds(pl.multiple_of(first, FEW), FEW)
        for z, plane in enumerate(taps(layer, 0, maps, weights, reach, rows, halo)):
            centre[z, rows, :] = plane

    if not last:
        kept[...] = maps[-1][...].astype(jnp.bfloat16)
        return

    columns = pl.ds(pl.multiple_of(halo + member() * inner, inner), inner)
    kept[...] = sum(mix_of(params, j) * ref[:, :, columns].astype(jnp.float32) for j, ref in enumerate(maps))


def call(kernel, out_shape, scalars, arrays, scratch=(), cost=None):
    return pl.pallas_call(
        kernel,
        out_shape=out_shape,
        in_specs=[SMEM] * len(scalars) + [VMEM] * len(arrays),
        out_specs=jax.tree.map(lambda _: VMEM, out_shape),
        scratch_shapes=list(scratch),
        cost_estimate=cost,
    )(*scalars, *arrays)


def body(noisy, dilations, conv_weights, biases, mix_weights):
    layers = conv_weights.shape[0]
    depth, width, height = noisy.shape
    blocks, paired = lax.axis_size("gx"), lax.axis_size("gy") == 2
    halo = 0 if paired else height
    assert height >= DMAX and lax.axis_size("gy") % 2 == 0 and width % ROWS == 0 and layers > 1
    field = jax.ShapeDtypeStruct((depth, width, 2 * height), jnp.float32)
    wide = (depth, width, 2 * (height + halo))
    own_shape = jax.ShapeDtypeStruct(noisy.shape, jnp.float32)
    cost = pl.CostEstimate(flops=72 * depth * width * 2 * height, bytes_accessed=1 << 20, transcendentals=0)

    own, ahead, behind, packed, params, weights = pl.pallas_call(
        start_kernel,
        out_shape=(
            own_shape,
            own_shape,
            own_shape,
            pltpu.SMEM((1,), jnp.int32),
            pltpu.SMEM((3, layers + 1), jnp.float32),
            pltpu.SMEM(conv_weights.shape, jnp.float32),
        ),
        in_specs=[pl.BlockSpec(memory_space=pl.ANY)] * 5,
        out_specs=(VMEM, VMEM, VMEM, SMEM, SMEM, SMEM),
        scratch_shapes=[
            *(pltpu.SMEM(value.shape, value.dtype) for value in (dilations, biases, mix_weights)),
            pltpu.VMEM(noisy.shape, noisy.dtype),
            pltpu.SemaphoreType.DMA((5,)),
        ],
    )(dilations, biases, mix_weights, noisy, conv_weights)
    code = packed[0] + 1
    bits = branch_counts(width)[-1].bit_length()
    route = [(code >> (bits * layer)) & ((1 << bits) - 1) for layer in range(layers)]

    def beside(layer, weights, params, maps):
        last = layer == layers - 1
        shapes = (own_shape, own_shape) if last else (field, jax.ShapeDtypeStruct(wide, jnp.bfloat16))
        kernel = functools.partial(beside_kernel, layer, last, halo)
        return call(kernel, shapes, (weights, params), maps, cost=cost)

    def first_finish(came, weights, params, own):
        pair = pair_gather(own)
        if paired:
            pair = pltpu.with_memory_space_constraint(pair, pltpu.VMEM)
            shapes = (field, jax.ShapeDtypeStruct(wide, jnp.bfloat16))
            scratch = [pltpu.VMEM(field.shape, jnp.float32)]
            found = call(first_beside_kernel, shapes, (weights, params), (pair,), scratch=scratch, cost=cost)
        else:
            found = beside(0, weights, params, [widen(jnp.concatenate([pair[0], pair[1]], axis=-1))])
        return pair_gather(came), found

    def middle_finish(layer):
        return lambda came, weights, params, *maps: (pair_gather(came), beside(layer, weights, params, maps))

    def last_finish(came, weights, params, *maps):
        return came, beside(layers - 1, weights, params, maps)

    scalars = (weights, params)
    came, (centre, kept) = exchange([ahead, behind], first_finish, (*scalars, own), route[0], False)
    older = [kept]
    for layer in range(1, layers):
        last = layer == layers - 1
        sent_shapes = [own_shape] * 2 if last else [field]
        if layer == 1 and paired:
            newest, *sent = call(
                functools.partial(first_layer_kernel, blocks),
                (field, *sent_shapes),
                scalars,
                (came, centre, kept),
                scratch=[pltpu.VMEM(field.shape, jnp.float32)] * 2,
            )
        elif paired:
            newest, *sent = call(
                functools.partial(layer_kernel, layer, blocks),
                (field, *sent_shapes),
                scalars,
                (came, centre, *older),
            )
        else:
            if layer == 1:
                windows = call(functools.partial(windows_kernel, blocks), (field, field), (params,), (came,))
                above, below = (widen(window) for window in windows)
                newest = call(
                    functools.partial(first_map_kernel, halo), field, scalars, (above, below, centre)
                )
            else:
                newest = call(functools.partial(map_kernel, layer - 1, blocks), field, (params,), (came, centre))
            newest = widen(newest)
            sent = call(
                functools.partial(sent_kernel, layer, halo), tuple(sent_shapes), scalars, (*older, newest)
            )
        finish = last_finish if last else middle_finish(layer)
        came, (centre, kept) = exchange(
            list(sent), finish, (*scalars, *older, newest), route[layer], last
        )
        older.append(kept)
    return call(
        functools.partial(last_kernel, layers, blocks),
        jax.ShapeDtypeStruct(noisy.shape, jnp.bfloat16),
        (params,),
        (came, centre, kept),
    )


def solution(mesh):
    return jax.shard_map(
        body,
        mesh=mesh,
        in_specs=(P(None, "gx", "gy"), P(), P(), P(), P()),
        out_specs=P(None, "gx", "gy"),
        check_vma=False,
    )
```
